32 devices in a mesh: sect: 4 (over x, core), lat: 2 (over y), var: 4 (over z).
Axes of the slice: x: 2, y: 2, z: 4, core: 2. Of those that a mesh axis runs over, the one named last changes fastest.
Arguments:
- patches: bfloat16 [16, 16, 256, 128], P(('sect', 'var'), 'lat'), may hold values from -6 to 6
- embed_weight: bfloat16 [16, 128, 512], P(('sect', 'var')), may hold values from -0.1875 to 0.1875
- qkv_weight: bfloat16 [2, 512, 3, 512], P(None, None, None, 'var'), may hold values from -0.25 to 0.25
- out_weight: bfloat16 [2, 512, 512], P(None, 'var'), may hold values from -2 to 2
- mlp_in_weight: bfloat16 [2, 512, 2048], P(None, None, 'var'), may hold values from -0.25 to 0.25
- mlp_out_weight: bfloat16 [2, 2048, 512], P(None, 'var'), may hold values from -2 to 2
- logit_scale: float32 [2, 8], P(None, 'var'), may hold values from 3 to 30
- norm_gain: float32 [2, 2, 512], P(None, None, 'var'), may hold values from 0.1 to 1.9
- norm_bias: float32 [2, 2, 512], P(None, None, 'var'), may hold values from -2.5 to 2.5
- decode_weight: bfloat16 [16, 512, 128], P(('sect', 'var')), may hold values from -0.25 to 0.25
- shifts: int32 [2, 2], replicated, may hold values from 1 to 7
Outputs:
- decoded: bfloat16 [16, 16, 256, 128], P(('sect', 'var'), 'lat')
The draws below stay inside these ranges and needn't reach their ends.
All inputs are finite; a program needn't handle non-finite values.
Results may differ from the reference program's by a relative error of at most 0.034.
Values may be sent and summed in bfloat16 or wider, within the bound.
A program may use at most 128 MiB of HBM per device.

```python
import math
import jax
import jax.numpy as jnp
from jax import lax

D = 512
HEADS = 8
HD = 64
FFN = 2048
PD = 128
WL = 8
WW = 16
LAYERS = 2
NLAT = 16
NLON = 256
NVAR = 16


def ramped_weight(key, rows):
    entries = jnp.clip(jax.random.normal(key, (LAYERS, rows, D), jnp.float32), -4.0, 4.0)
    ratio = 10.0
    place = jnp.arange(D, dtype=jnp.float32) / (D - 1) - 0.5
    column_scale = jnp.exp(math.log(ratio) * place)
    values = entries * column_scale[None, None, :] * rows ** (-0.5)
    return jnp.clip(values, -2.0, 2.0).astype(jnp.bfloat16)


def draw_out_weight(key, part):
    return ramped_weight(jax.random.fold_in(key, 101), HEADS * HD)


def draw_mlp_out_weight(key, part):
    return ramped_weight(jax.random.fold_in(key, 202), FFN)


def touch_ends(values, rng, least, largest):
    dims = values.shape
    index_at = [jax.random.randint(jax.random.fold_in(rng, axis), (), 0, dims[axis]) for axis in range(len(dims))]
    values = values.at[tuple(index_at)].set(least)
    longest = dims.index(max(dims))
    index_at[longest] = (index_at[longest] + 1) % dims[longest]
    return values.at[tuple(index_at)].set(largest)


def raised(values, rng, source, target, parts, factor):
    def block_of(axis_at):
        return (jnp.arange(values.shape[axis_at]) // (values.shape[axis_at] // parts)).reshape((-1,) + (1,) * (values.ndim - 1 - axis_at))

    first = jax.random.permutation(rng, parts)[block_of(target)]
    second = (block_of(target) + parts // 2) % parts
    return jnp.where((block_of(source) == first) | (block_of(source) == second), factor * values, values)


def levels(stream_key, dims, pieces, least, high):
    gain, own = 1.0, jax.random.fold_in(stream_key, 6)
    for position, parts in pieces:
        heights = jnp.exp(jax.random.uniform(jax.random.fold_in(own, position), (parts,), jnp.float32, least / len(pieces), high / len(pieces)))
        gain = gain * jnp.repeat(heights, dims[position] // parts).reshape([-1 if axis == position else 1 for axis in range(len(dims))])
    return gain


def gaussian(own_key, shape, deviation, reach, cuts=(), kind=jnp.bfloat16):
    gain = levels(own_key, shape, cuts, -0.22, 0.18) if cuts else 1.0
    drawn = jax.random.normal(own_key, shape, jnp.float32) * deviation * gain
    return jnp.minimum(jnp.maximum(drawn, -reach), reach).astype(kind)


def heavy_noise(rng, extent, width, limit, split, heavy, kind=jnp.bfloat16):
    values = width * jax.random.normal(rng, extent, jnp.float32)
    if split:
        values = values * levels(rng, extent, split, -0.22, 0.18)
    return jnp.clip(raised(values, jax.random.fold_in(rng, 3), *heavy), -limit, limit).astype(kind)


def setup_inputs(seed: int = 0) -> dict:
    splits = jax.random.split(jax.random.key(seed), 12)
    return {
        "patches": gaussian(splits[0], (NVAR, NLAT, NLON, PD), 1.0, 6.0, ((0, 16), (1, 2))),
        "embed_weight": heavy_noise(splits[1], (NVAR, PD, D), (PD * NVAR) ** -0.5, 0.1875, ((0, 16),), (0, 2, 16, 2.0)),
        "qkv_weight": gaussian(splits[2], (LAYERS, D, 3, HEADS * HD), D ** -0.5, 0.25, ((3, 4),)),
        "out_weight": draw_out_weight(jax.random.fold_in(splits[11], 71), 0),
        "mlp_in_weight": gaussian(splits[4], (LAYERS, D, FFN), D ** -0.5, 0.25, ((2, 4),)),
        "mlp_out_weight": draw_mlp_out_weight(jax.random.fold_in(splits[11], 71), 0),
        "logit_scale": jnp.clip(jnp.exp(math.log(30.0) - 2.3025851 * jax.random.uniform(splits[6], (LAYERS, HEADS), jnp.float32) ** levels(splits[6], (LAYERS, HEADS), ((1, 4),), -0.2, 0.2)), 3.0, 30.0),
        "norm_gain": jnp.clip(1.0 + 0.18 * jax.random.normal(splits[7], (LAYERS, 2, D), jnp.float32), 0.1, 1.9),
        "norm_bias": gaussian(splits[8], (LAYERS, 2, D), 0.4, 2.5, ((2, 4),), jnp.float32),
        "decode_weight": gaussian(splits[9], (NVAR, D, PD), D ** -0.5, 0.25, ((0, 16),)),
        "shifts": touch_ends(jax.random.randint(splits[10], (LAYERS, 2), 1, WL), jax.random.fold_in(splits[10], 1), 1, WL - 1).astype(jnp.int32),
    }


epsilon = 1e-06

def unit_norm(vector_rows):
    return vector_rows * lax.rsqrt(lax.optimization_barrier(jnp.sum(vector_rows * vector_rows, axis=-1, keepdims=True)) + epsilon)

def to_windows(frame, win_rows, win_cols):
    shaped = frame.reshape(win_rows, WL, win_cols, WW, HEADS, HD)
    return shaped.transpose(0, 2, 1, 3, 4, 5).reshape(win_rows, win_cols, WL * WW, HEADS, HD)

def post_norm(stream, mixed_sum, gain_row, bias_row):
    avg_feat = lax.optimization_barrier(jnp.sum(mixed_sum, axis=-1, keepdims=True)) / D
    variance = lax.optimization_barrier(jnp.sum(mixed_sum * mixed_sum, axis=-1, keepdims=True)) / D - avg_feat * avg_feat
    normed = (mixed_sum - avg_feat) * lax.rsqrt(variance + 1e-05)
    return (stream.astype(jnp.float32) + gain_row * normed + bias_row).astype(jnp.bfloat16)

def layer_step(stream, wqkv, wout, w_in, w_out, head_scale, gain_row, bias_row, shift_lat, shift_lon):
    projected = jnp.dot(stream.reshape(NLAT * NLON, D), wqkv.reshape(D, 3 * HEADS * HD), preferred_element_type=jnp.float32)
    projected = projected.reshape(NLAT, NLON, 3, HEADS, HD)
    queries = unit_norm(projected[:, :, 0]).astype(jnp.bfloat16)
    key_vals = unit_norm(projected[:, :, 1]).astype(jnp.bfloat16)
    values = projected[:, :, 2].astype(jnp.bfloat16)
    frame_rows = NLAT + WL
    win_rows = frame_rows // WL
    win_cols = NLON // WW

    def framed(array):
        padded = jnp.pad(array, ((WL, WL), (0, 0), (0, 0), (0, 0)))
        sliced = lax.dynamic_slice_in_dim(padded, shift_lat, frame_rows, 0)
        return jnp.roll(sliced, -shift_lon, axis=1)
    q_win = to_windows(framed(queries), win_rows, win_cols).astype(jnp.float32)
    k_win = to_windows(framed(key_vals), win_rows, win_cols).astype(jnp.float32)
    v_win = to_windows(framed(values), win_rows, win_cols).astype(jnp.float32)
    scores = jnp.einsum('wnqhe,wnkhe->wnhqk', q_win, k_win) * head_scale[:, None, None]
    global_row = jnp.arange(frame_rows, dtype=jnp.int32) + shift_lat - WL
    usable = (global_row >= 0) & (global_row < NLAT)
    usable = jnp.broadcast_to(usable.reshape(win_rows, 1, WL, 1), (win_rows, win_cols, WL, WW)).reshape(win_rows, win_cols, 1, 1, WL * WW)
    scores = jnp.where(usable, scores, -1e+30)
    top = lax.optimization_barrier(jnp.max(scores, axis=-1, keepdims=True))
    expo = jnp.exp(scores - top)
    weights = (expo / lax.optimization_barrier(jnp.sum(expo, axis=-1, keepdims=True))).astype(jnp.bfloat16)
    attended = jnp.einsum('wnhqk,wnkhe->wnqhe', weights.astype(jnp.float32), v_win).astype(jnp.bfloat16)
    attended = attended.reshape(win_rows, win_cols, WL, WW, HEADS * HD).transpose(0, 2, 1, 3, 4).reshape(frame_rows, NLON, HEADS * HD)
    attended = jnp.roll(attended, shift_lon, axis=1)
    attended = lax.dynamic_slice_in_dim(attended, WL - shift_lat, NLAT, 0)
    mixed_sum = jnp.dot(attended.reshape(NLAT * NLON, HEADS * HD), wout, preferred_element_type=jnp.float32).reshape(NLAT, NLON, D)
    attn_stream = post_norm(stream, mixed_sum, gain_row[0], bias_row[0])
    hidden = jax.nn.gelu(jnp.dot(attn_stream.reshape(NLAT * NLON, D), w_in, preferred_element_type=jnp.float32)).astype(jnp.bfloat16)
    fed = jnp.dot(hidden, w_out, preferred_element_type=jnp.float32).reshape(NLAT, NLON, D)
    return post_norm(attn_stream, fed, gain_row[1], bias_row[1])

def reference(patches, embed_weight, qkv_weight, out_weight, mlp_in_weight, mlp_out_weight, logit_scale, norm_gain, norm_bias, decode_weight, shifts):
    flat_rows = jnp.transpose(patches, (1, 2, 0, 3)).reshape(NLAT * NLON, NVAR * PD)
    stream = jnp.dot(flat_rows, embed_weight.reshape(NVAR * PD, D), preferred_element_type=jnp.float32)
    stream = stream.reshape(NLAT, NLON, D).astype(jnp.bfloat16)
    for layer_id in range(LAYERS):
        stream = layer_step(stream, qkv_weight[layer_id], out_weight[layer_id], mlp_in_weight[layer_id], mlp_out_weight[layer_id], logit_scale[layer_id], norm_gain[layer_id], norm_bias[layer_id], shifts[layer_id, 0], shifts[layer_id, 1])
    table = jnp.transpose(decode_weight, (1, 0, 2)).reshape(D, NVAR * PD)
    decoded = jnp.dot(stream.reshape(NLAT * NLON, D), table, preferred_element_type=jnp.float32).astype(jnp.bfloat16)
    return jnp.transpose(decoded.reshape(NLAT, NLON, NVAR, PD), (2, 0, 1, 3))
```

```python
import functools
import jax
import jax.numpy as jnp
from jax import lax
from jax.experimental import pallas as pl
from jax.experimental.pallas import tpu as pltpu
from jax.sharding import PartitionSpec as P

WL = 8
WW = 16
HD = 64
MESH = pl.DeviceIdType.MESH

epsilon = 1e-06


def extended(array, sides, width, wrap):
    for axis, dim in sides:
        size, length = (lax.axis_size(axis), array.shape[dim])
        up = [(i, (i + 1) % size) for i in range(size if wrap else size - 1)]
        down = [(j, i) for i, j in up]
        last = lax.slice_in_dim(array, length - width, length, axis=dim)
        initial = lax.slice_in_dim(array, 0, width, axis=dim)
        before = lax.ppermute(last, axis, up)
        after = lax.ppermute(initial, axis, down)
        array = jnp.concatenate([before, array, after], axis=dim)
    return array


def to_windows(frame, win_rows, win_cols, heads_local, head_dim):
    shaped = frame.reshape(win_rows, WL, win_cols, WW, heads_local, head_dim)
    return shaped.transpose(0, 2, 1, 3, 4, 5).reshape(
        win_rows, win_cols, WL * WW, heads_local, head_dim
    )


def attend(queries, paired, head_scale, shift_lat, shift_lon, heads_local, head_dim):
    lat_rows, lon_cols, head_cols = queries.shape
    query_pad = jnp.pad(queries, ((WL, WL), (WW, WW), (0, 0)))
    frame_rows = lat_rows + WL
    frame_cols = lon_cols + WW
    win_rows = frame_rows // WL
    win_cols = frame_cols // WW
    q_frame = lax.dynamic_slice(
        query_pad, (shift_lat, shift_lon, 0), (frame_rows, frame_cols, head_cols)
    )
    kv_frame = lax.dynamic_slice(
        paired, (shift_lat, shift_lon, 0), (frame_rows, frame_cols, 2 * head_cols)
    )
    q_win = to_windows(q_frame, win_rows, win_cols, heads_local, head_dim)
    k_win = to_windows(kv_frame[:, :, :head_cols], win_rows, win_cols, heads_local, head_dim)
    v_win = to_windows(kv_frame[:, :, head_cols:], win_rows, win_cols, heads_local, head_dim)
    scores = (
        jnp.einsum("wnqhe,wnkhe->wnhqk", q_win, k_win, preferred_element_type=jnp.float32)
        * head_scale[:, None, None]
    )
    lat_total = lat_rows * lax.axis_size("lat")
    global_row = (
        lax.axis_index("lat") * lat_rows - WL + shift_lat + jnp.arange(frame_rows, dtype=jnp.int32)
    )
    usable = (global_row >= 0) & (global_row < lat_total)
    usable = jnp.broadcast_to(
        usable.reshape(win_rows, 1, WL, 1), (win_rows, win_cols, WL, WW)
    ).reshape(win_rows, win_cols, 1, 1, WL * WW)
    scores = jnp.where(usable, scores, -1e30)
    top = jnp.max(scores, axis=-1, keepdims=True)
    expo = jnp.exp(scores - top)
    weights = (expo / jnp.sum(expo, axis=-1, keepdims=True)).astype(jnp.bfloat16)
    attended = jnp.einsum(
        "wnhqk,wnkhe->wnqhe", weights, v_win, preferred_element_type=jnp.float32
    ).astype(jnp.bfloat16)
    attended = (
        attended.reshape(win_rows, win_cols, WL, WW, head_cols)
        .transpose(0, 2, 1, 3, 4)
        .reshape(frame_rows, frame_cols, head_cols)
    )
    return lax.dynamic_slice(
        attended, (WL - shift_lat, WW - shift_lon, 0), (lat_rows, lon_cols, head_cols)
    )


def dot(a, b):
    return jnp.dot(a, b, preferred_element_type=jnp.float32)


def greet(axes):
    barrier = pltpu.get_barrier_semaphore()
    total = 0
    for axis in axes:
        size = lax.axis_size(axis)
        me = lax.axis_index(axis)
        for d in range(1, size):
            pl.semaphore_signal(
                barrier, inc=1, device_id={axis: lax.rem(me + d, size)}, device_id_type=MESH
            )
            total += 1
    pl.semaphore_wait(barrier, total)


def send(src, dst, sems, phase, d, axis, target):
    send_sem, recv_sem = sems
    copy = pltpu.make_async_remote_copy(
        src_ref=src,
        dst_ref=dst,
        send_sem=send_sem.at[phase, d],
        recv_sem=recv_sem.at[phase, d],
        device_id={axis: target},
        device_id_type=MESH,
    )
    copy.start()
    return copy


def ring(axis):
    size = lax.axis_size(axis)
    me = lax.axis_index(axis)
    after = [lax.rem(me + d, size) for d in range(size)]
    before = [lax.rem(me + size - d, size) for d in range(size)]
    return size, me, after, before


def head_unit(x):
    lane = lax.broadcasted_iota(jnp.int32, x.shape, 1)
    square = x * x
    inverse = jnp.zeros_like(x)
    for head in range(x.shape[1] // HD):
        mine = (lane >= head * HD) & (lane < (head + 1) * HD)
        total = jnp.sum(jnp.where(mine, square, 0.0), axis=1, keepdims=True)
        inverse = jnp.where(mine, lax.rsqrt(total + epsilon), inverse)
    return x * inverse


def project_chunk(x, wqkv_ref, q_ref, kv_ref, owner):
    rows, cols = x.shape[0], q_ref.shape[1]
    projected = dot(x, wqkv_ref[...])
    at = pl.ds(pl.multiple_of(owner * rows, rows), rows)
    q_ref[at, :] = head_unit(projected[:, :cols]).astype(jnp.bfloat16)
    kv_ref[at, :cols] = head_unit(projected[:, cols : 2 * cols]).astype(jnp.bfloat16)
    kv_ref[at, cols:] = projected[:, 2 * cols :].astype(jnp.bfloat16)


def norm_add(stream, x, gain, bias):
    width = x.shape[1]
    mean = jnp.sum(x, axis=1, keepdims=True) / width
    variance = jnp.sum(x * x, axis=1, keepdims=True) / width - mean * mean
    normed = (x - mean) * lax.rsqrt(variance + 1e-05)
    return (stream.astype(jnp.float32) + gain * normed + bias).astype(jnp.bfloat16)


def embed_kernel(
    patches, table, params, wqkv, q_ref, kv_ref, x_ref, params_ref,
    patch_in, table_in, params_in, part, part_in, full, send_sem, recv_sem,
):
    sems = (send_sem, recv_sem)
    sects, my_sect, to_sect, _ = ring("sect")
    vars_, my_var, to_var, from_var = ring("var")
    lat_rows, lon_total, depth = patches.shape
    cols = lon_total // sects
    rows = full.shape[1]
    greet(("sect", "var"))
    copies = []
    moved = []
    for d in range(1, sects):
        t = to_sect[d]
        moved.append(send(table, table_in.at[d - 1], sems, 0, d, "sect", t))
        moved.append(
            send(
                patches.at[:, pl.ds(pl.multiple_of(t * cols, cols), cols), :],
                patch_in.at[d - 1], sems, 1, d, "sect", t,
            )
        )
    params_in[my_var] = params[...]
    for d in range(1, vars_):
        copies.append(
            send(params, params_in.at[my_var], sems, 2, d, "var", to_var[d])
        )
    for copy in moved:
        copy.wait()
    weights = jnp.concatenate([table[...]] + [table_in[d] for d in range(sects - 1)], axis=0)
    per = rows // cols

    def partial_of(owner):
        lat = pl.ds(owner * per, per)
        own = patches[lat, pl.ds(pl.multiple_of(my_sect * cols, cols), cols), :]
        blocks = [own] + [patch_in[d, lat] for d in range(sects - 1)]
        x = jnp.concatenate([b.reshape(rows, depth) for b in blocks], axis=1)
        return dot(x, weights)

    outgoing = []
    for d in range(1, vars_):
        part[d - 1] = partial_of(to_var[d]).astype(jnp.bfloat16)
        outgoing.append(send(part.at[d - 1], part_in.at[d - 1], sems, 3, d, "var", to_var[d]))
    total = partial_of(my_var)
    for d in range(1, vars_):
        outgoing[d - 1].wait()
        total = total + part_in[d - 1].astype(jnp.float32)
    full[my_var] = total.astype(jnp.bfloat16)
    gather_project(full, wqkv, q_ref, kv_ref, sems, 4)
    x_ref[...] = full[...]
    for copy in copies:
        copy.wait()
    params_ref[...] = params_in[...]


def gather_project(full, wqkv, q_ref, kv_ref, sems, phase):
    vars_, my_var, to_var, from_var = ring("var")
    outgoing = [
        send(full.at[my_var], full.at[my_var], sems, phase, d, "var", to_var[d])
        for d in range(1, vars_)
    ]
    project_chunk(full[my_var], wqkv, q_ref, kv_ref, my_var)
    for d in range(1, vars_):
        outgoing[d - 1].wait()
        project_chunk(full[from_var[d]], wqkv, q_ref, kv_ref, from_var[d])


def layer_body(
    layer, attended, wout, x_ref, params, w_in, w_out, part, part_in, mid, back, back_in, full, sems
):
    vars_, my_var, to_var, from_var = ring("var")
    rows = mid.shape[1]

    def chosen(kind, position):
        index = (kind * 2 + layer) * 2 + position
        return jnp.concatenate([params[v, index : index + 1, :] for v in range(vars_)], axis=1)

    def mixed_of(owner):
        at = pl.ds(pl.multiple_of(owner * rows, rows), rows)
        return dot(attended[at, :], wout[...])

    def fed_of(x):
        hidden = jax.nn.gelu(dot(x, w_in[...]), approximate=True).astype(jnp.bfloat16)
        return dot(hidden, w_out[...])

    outgoing = []
    for d in range(1, vars_):
        part[d - 1] = mixed_of(to_var[d]).astype(jnp.bfloat16)
        outgoing.append(send(part.at[d - 1], part_in.at[d - 1], sems, 0, d, "var", to_var[d]))
    total = mixed_of(my_var)
    for d in range(1, vars_):
        outgoing[d - 1].wait()
        total = total + part_in[d - 1].astype(jnp.float32)
    mid[my_var] = norm_add(x_ref[my_var], total, chosen(0, 0), chosen(1, 0))
    outgoing = [
        send(mid.at[my_var], mid.at[my_var], sems, 1, d, "var", to_var[d])
        for d in range(1, vars_)
    ]
    total = fed_of(mid[my_var])
    returned = []
    for d in range(1, vars_):
        outgoing[d - 1].wait()
        back[d - 1] = fed_of(mid[from_var[d]]).astype(jnp.bfloat16)
        returned.append(send(back.at[d - 1], back_in.at[d - 1], sems, 2, d, "var", from_var[d]))
    for d in range(1, vars_):
        returned[d - 1].wait()
        total = total + back_in[d - 1].astype(jnp.float32)
    full[my_var] = norm_add(mid[my_var], total, chosen(0, 1), chosen(1, 1))


def layer_kernel(
    layer, attended, wout, x_ref, params, w_in, w_out, wqkv, q_ref, kv_ref, out_ref,
    part, part_in, mid, back, back_in, full, send_sem, recv_sem,
):
    sems = (send_sem, recv_sem)
    greet(("var",))
    layer_body(
        layer, attended, wout, x_ref, params, w_in, w_out, part, part_in, mid, back, back_in, full, sems
    )
    gather_project(full, wqkv, q_ref, kv_ref, sems, 3)
    out_ref[...] = full[...]


def last_kernel(
    layer, attended, wout, x_ref, params, w_in, w_out, table, out_ref,
    part, part_in, mid, back, back_in, full, table_in, made, landed, send_sem, recv_sem,
):
    sems = (send_sem, recv_sem)
    sects, my_sect, to_sect, from_sect = ring("sect")
    vars_, my_var, to_var, from_var = ring("var")
    rows = full.shape[1]
    lat_rows, lon_total, depth = out_ref.shape
    cols = lon_total // sects
    per = rows // cols
    greet(("sect", "var"))
    tables = [
        send(table, table_in.at[d - 1], sems, 4, d, "sect", to_sect[d]) for d in range(1, sects)
    ]
    layer_body(
        layer, attended, wout, x_ref, params, w_in, w_out, part, part_in, mid, back, back_in, full, sems
    )
    outgoing = [
        send(full.at[my_var], full.at[my_var], sems, 3, d, "var", to_var[d])
        for d in range(1, vars_)
    ]
    for copy in tables:
        copy.wait()
    weights = jnp.concatenate([table[...]] + [table_in[d] for d in range(sects - 1)], axis=1)
    for k in range(vars_):
        if k:
            outgoing[k - 1].wait()
        owner = from_var[k]
        decoded = dot(full[owner], weights).astype(jnp.bfloat16)
        for d in range(sects):
            made[d, pl.ds(owner * per, per)] = decoded[:, d * depth : (d + 1) * depth].reshape(
                per, cols, depth
            )
    copies = []
    for d in range(1, sects):
        copies.append(
            send(made.at[d], landed.at[sects - d], sems, 5, d, "sect", from_sect[d])
        )
    out_ref[:, pl.ds(pl.multiple_of(my_sect * cols, cols), cols), :] = made[0]
    for d in range(1, sects):
        copies[d - 1].wait()
        block = to_sect[d]
        out_ref[:, pl.ds(pl.multiple_of(block * cols, cols), cols), :] = landed[sects - d]


def per_device(
    patches,
    embed_weight,
    qkv_weight,
    out_weight,
    mlp_in_weight,
    mlp_out_weight,
    logit_scale,
    norm_gain,
    norm_bias,
    decode_weight,
    shifts,
):
    _, lat_rows, lon_total, patch_dim = patches.shape
    width = embed_weight.shape[2]
    layers, _, _, head_cols = qkv_weight.shape
    sects, vars_ = lax.axis_size("sect"), lax.axis_size("var")
    cols = lon_total // sects
    tokens = lat_rows * cols
    rows = tokens // vars_
    hidden = mlp_in_weight.shape[2]
    bf = jnp.bfloat16
    vmem = pl.BlockSpec(memory_space=pltpu.VMEM)
    wqkv = [qkv_weight[layer].reshape(width, 3 * head_cols) for layer in range(layers)]
    params = jnp.concatenate(
        [norm_gain.reshape(2 * layers, -1), norm_bias.reshape(2 * layers, -1)], axis=0
    )

    def call(kernel, cid, outs, scratch, phases, *args):
        return pl.pallas_call(
            kernel,
            out_shape=outs,
            in_specs=[vmem] * len(args),
            out_specs=jax.tree.map(lambda _: vmem, outs),
            scratch_shapes=scratch
            + [pltpu.SemaphoreType.DMA((phases, 4)), pltpu.SemaphoreType.DMA((phases, 4))],
            compiler_params=pltpu.CompilerParams(
                collective_id=cid, has_side_effects=True, vmem_limit_bytes=40 * 1024 * 1024
            ),
        )(*args)

    qkv_outs = [
        jax.ShapeDtypeStruct((tokens, head_cols), bf),
        jax.ShapeDtypeStruct((tokens, 2 * head_cols), bf),
        jax.ShapeDtypeStruct((vars_, rows, width), bf),
    ]
    q, kv, x, params = call(
        embed_kernel, 0,
        qkv_outs + [jax.ShapeDtypeStruct((vars_,) + params.shape, jnp.float32)],
        [
            pltpu.VMEM((sects - 1, lat_rows, cols, patch_dim), bf),
            pltpu.VMEM((sects - 1, patch_dim, width), bf),
            pltpu.VMEM((vars_,) + params.shape, jnp.float32),
            pltpu.VMEM((vars_ - 1, rows, width), bf),
            pltpu.VMEM((vars_ - 1, rows, width), bf),
            pltpu.VMEM((vars_, rows, width), bf),
        ],
        5, patches[0], embed_weight[0], params, wqkv[0],
    )
    slots = [
        pltpu.VMEM((vars_ - 1, rows, width), bf),
        pltpu.VMEM((vars_ - 1, rows, width), bf),
        pltpu.VMEM((vars_, rows, width), bf),
        pltpu.VMEM((vars_ - 1, rows, width), bf),
        pltpu.VMEM((vars_ - 1, rows, width), bf),
        pltpu.VMEM((vars_, rows, width), bf),
    ]
    for layer in range(layers):
        paired = kv.reshape(lat_rows, cols, 2 * head_cols)
        paired = extended(paired, (("lat", 0),), WL, False)
        paired = extended(paired, (("sect", 1),), WW, True)
        attended = attend(
            q.reshape(lat_rows, cols, head_cols), paired, logit_scale[layer],
            shifts[layer, 0], shifts[layer, 1], head_cols // HD, HD,
        ).reshape(tokens, head_cols)
        args = (
            attended, out_weight[layer], x, params, mlp_in_weight[layer], mlp_out_weight[layer]
        )
        if layer + 1 < layers:
            q, kv, x = call(
                functools.partial(layer_kernel, layer), 1 + layer, qkv_outs, slots, 4,
                *args, wqkv[layer + 1],
            )
    out = call(
        functools.partial(last_kernel, layers - 1), layers,
        jax.ShapeDtypeStruct((lat_rows, lon_total, patch_dim), bf),
        slots
        + [
            pltpu.VMEM((sects - 1, width, patch_dim), bf),
            pltpu.VMEM((sects, lat_rows, cols, patch_dim), bf),
            pltpu.VMEM((sects, lat_rows, cols, patch_dim), bf),
        ],
        6, *args, decode_weight[0],
    )
    return out[None]


def solution(mesh):
    return jax.shard_map(
        per_device,
        mesh=mesh,
        in_specs=(
            P(("sect", "var"), "lat", None, None),
            P(("sect", "var"), None, None),
            P(None, None, None, "var"),
            P(None, "var", None),
            P(None, None, "var"),
            P(None, "var", None),
            P(None, "var"),
            P(None, None, "var"),
            P(None, None, "var"),
            P(("sect", "var"), None, None),
            P(),
        ),
        out_specs=P(("sect", "var"), "lat", None, None),
        check_vma=False,
    )
```

```python
import jax
import jax.numpy as jnp
from jax import lax
from jax.experimental import pallas as pl
from jax.experimental.pallas import tpu as pltpu
from jax.sharding import PartitionSpec as P

WL = 8
WW = 16
HD = 64
MESH = pl.DeviceIdType.MESH

epsilon = 1e-06


def dot(a, b):
    return jnp.dot(a, b, preferred_element_type=jnp.float32)


def send(src, dst, sems, phase, d, axis, target):
    send_sem, recv_sem = sems
    copy = pltpu.make_async_remote_copy(
        src_ref=src,
        dst_ref=dst,
        send_sem=send_sem.at[phase, d],
        recv_sem=recv_sem.at[phase, d],
        device_id={axis: target},
        device_id_type=MESH,
    )
    copy.start()
    return copy


def ring(axis):
    size = lax.axis_size(axis)
    me = lax.axis_index(axis)
    after = [lax.rem(me + d, size) for d in range(size)]
    before = [lax.rem(me + size - d, size) for d in range(size)]
    return size, me, after, before


def head_unit(x):
    lane = lax.broadcasted_iota(jnp.int32, x.shape, 1)
    square = x * x
    inverse = jnp.zeros_like(x)
    for head in range(x.shape[1] // HD):
        mine = (lane >= head * HD) & (lane < (head + 1) * HD)
        total = jnp.sum(jnp.where(mine, square, 0.0), axis=1, keepdims=True)
        inverse = jnp.where(mine, lax.rsqrt(total + epsilon), inverse)
    return x * inverse


def project_chunk(x, wqkv, q_ref, kv_ref, owner):
    rows, cols = x.shape[0], q_ref.shape[2]
    lon = q_ref.shape[1] - 2 * WW
    per = rows // lon
    projected = dot(x, wqkv)
    lat = pl.ds(WL + owner * per, per)
    inner = slice(WW, WW + lon)
    q_ref[lat, inner, :] = head_unit(projected[:, :cols]).reshape(per, lon, cols)
    keys = head_unit(projected[:, cols : 2 * cols])
    paired = jnp.concatenate([keys, projected[:, 2 * cols :]], axis=1).astype(jnp.bfloat16)
    kv_ref[lat, inner, :] = paired.reshape(per, lon, 2 * cols)


def norm_add(stream, x, gain, bias):
    width = x.shape[1]
    mean = jnp.sum(x, axis=1, keepdims=True) / width
    variance = jnp.sum(x * x, axis=1, keepdims=True) / width - mean * mean
    normed = (x - mean) * lax.rsqrt(variance + 1e-05)
    return (stream.astype(jnp.float32) + gain * normed + bias).astype(jnp.bfloat16)


def gather_project(full, wqkv, q_ref, kv_ref, sems, phase):
    vars_, my_var, to_var, from_var = ring("var")
    outgoing = [
        send(full.at[my_var], full.at[my_var], sems, phase, d, "var", to_var[d])
        for d in range(1, vars_)
    ]
    project_chunk(full[my_var], wqkv, q_ref, kv_ref, my_var)
    for d in range(1, vars_):
        outgoing[d - 1].wait()
        project_chunk(full[from_var[d]], wqkv, q_ref, kv_ref, from_var[d])


def lat_neighbours():
    size, me = lax.axis_size("lat"), lax.axis_index("lat")
    return {1: me < size - 1, -1: me > 0}


def halo(kv_ref, send_sem, recv_sem):
    sects, my_sect = lax.axis_size("sect"), lax.axis_index("sect")
    my_lat = lax.axis_index("lat")
    lon = kv_ref.shape[1] - 2 * WW
    exists = lat_neighbours()
    taken = {0: slice(WW, WW + lon), 1: slice(lon, WW + lon), -1: slice(WW, 2 * WW)}
    placed = {0: slice(WW, WW + lon), 1: slice(0, WW), -1: slice(WW + lon, 2 * WW + lon)}
    landing = {0: slice(WL, 2 * WL), 1: slice(0, WL), -1: slice(2 * WL, 3 * WL)}
    copies = []
    index = 0
    for dl in (1, -1, 0):
        for ds in (0, 1, -1):
            if dl == 0 and ds == 0:
                continue
            target = {"sect": lax.rem(my_sect + ds + sects, sects), "lat": my_lat + dl}
            copy = pltpu.make_async_remote_copy(
                src_ref=kv_ref.at[WL : 2 * WL, taken[ds], :],
                dst_ref=kv_ref.at[landing[dl], placed[ds], :],
                send_sem=send_sem.at[index],
                recv_sem=recv_sem.at[index],
                device_id=target,
                device_id_type=MESH,
            )
            index += 1
            copies.append((dl, copy))
            if dl:
                pl.when(exists[dl])(copy.start)
            else:
                copy.start()
    for dl, copy in copies:
        if dl:
            pl.when(exists[dl])(copy.wait_send)
            pl.when(exists[-dl])(copy.wait_recv)
        else:
            copy.wait()


def attention(layer, shifts, scales, q_ref, kv_ref, wide, q_shifted, kv_shifted, framed, attended):
    lat_rows, lon = WL, q_ref.shape[1] - 2 * WW
    cols = q_ref.shape[2]
    a, b = shifts[layer, 0], shifts[layer, 1]
    my_lat, lats = lax.axis_index("lat"), lax.axis_size("lat")
    wide[...] = kv_ref[...].astype(jnp.float32)
    frame_rows, frame_cols = lat_rows + WL, lon + WW

    def turned(row, step, length):
        return pltpu.roll(row, row.shape[0] - step, 0)[:length].astype(jnp.bfloat16)

    for r in range(frame_rows):
        kv_shifted[r] = turned(wide[a + r], b, frame_cols)
        q_shifted[r] = turned(q_ref[a + r], b, frame_cols)
    lane = lax.broadcasted_iota(jnp.int32, (WL * WW, cols), 1)
    key_row = lax.broadcasted_iota(jnp.int32, (WL * WW, WL * WW), 1) // WW
    heads = cols // HD

    @pl.loop(0, frame_cols // WW)
    def _(n):
        at = pl.ds(pl.multiple_of(n * WW, WW), WW)
        for m in range(frame_rows // WL):
            rows = slice(m * WL, (m + 1) * WL)
            queries = q_shifted[rows, at, :].reshape(WL * WW, cols)
            paired = kv_shifted[rows, at, :].reshape(WL * WW, 2 * cols)
            keys, values = paired[:, :cols], paired[:, cols:]
            place = my_lat * lat_rows - WL + a + m * WL + key_row
            usable = (place >= 0) & (place < lats * lat_rows)
            result = jnp.zeros((WL * WW, cols), jnp.float32)
            for h in range(heads):
                mine = (lane >= h * HD) & (lane < (h + 1) * HD)
                part = jnp.where(mine, queries, jnp.zeros_like(queries))
                scores = lax.dot_general(
                    part, keys, (((1,), (1,)), ((), ())), preferred_element_type=jnp.float32
                )
                scale = scales[layer, h]
                expo = jnp.where(usable, jnp.exp((scores - 1.0) * scale), 0.0)
                total = jnp.sum(expo, axis=1, keepdims=True)
                weights = (expo / total).astype(jnp.bfloat16)
                result = jnp.where(mine, dot(weights, values), result)
            framed[rows, at, :] = result.reshape(WL, WW, cols)

    for r in range(lat_rows):
        attended[r * lon : (r + 1) * lon, :] = turned(framed[WL - a + r], WW - b, lon)


def feed(
    layer, attended, wout, x_ref, params, w_in, w_out, part, part_in, mid, back, back_in, full, sems
):
    vars_, my_var, to_var, from_var = ring("var")
    rows = mid.shape[1]

    def chosen(kind, position):
        index = (kind * 2 + layer) * 2 + position
        return jnp.concatenate([params[v, index : index + 1, :] for v in range(vars_)], axis=1)

    def mixed_of(owner):
        at = pl.ds(pl.multiple_of(owner * rows, rows), rows)
        return dot(attended[at, :], wout[layer])

    def fed_of(x):
        hidden = jax.nn.gelu(dot(x, w_in[layer]), approximate=True).astype(jnp.bfloat16)
        return dot(hidden, w_out[layer])

    first = 4 + 4 * layer
    outgoing = []
    for d in range(1, vars_):
        part[d - 1] = mixed_of(to_var[d]).astype(jnp.bfloat16)
        outgoing.append(send(part.at[d - 1], part_in.at[d - 1], sems, first, d, "var", to_var[d]))
    total = mixed_of(my_var)
    for d in range(1, vars_):
        outgoing[d - 1].wait()
        total = total + part_in[d - 1].astype(jnp.float32)
    mid[my_var] = norm_add(x_ref[my_var], total, chosen(0, 0), chosen(1, 0))
    outgoing = [
        send(mid.at[my_var], mid.at[my_var], sems, first + 1, d, "var", to_var[d])
        for d in range(1, vars_)
    ]
    total = fed_of(mid[my_var])
    returned = []
    for d in range(1, vars_):
        outgoing[d - 1].wait()
        back[d - 1] = fed_of(mid[from_var[d]]).astype(jnp.bfloat16)
        returned.append(
            send(back.at[d - 1], back_in.at[d - 1], sems, first + 2, d, "var", from_var[d])
        )
    for d in range(1, vars_):
        returned[d - 1].wait()
        total = total + back_in[d - 1].astype(jnp.float32)
    full[my_var] = norm_add(mid[my_var], total, chosen(0, 1), chosen(1, 1))


def whole_kernel(
    patches, table, wqkv, wout, w_in, w_out, scales, params, decode, shifts, out_ref,
    patch_in, table_in, params_in, part, part_in, full, mid, back, back_in,
    q_ref, kv_ref, wide, q_shifted, kv_shifted, framed, attended,
    decode_in, made, landed, send_sem, recv_sem, halo_send, halo_recv,
):
    sems = (send_sem, recv_sem)
    sects, my_sect, to_sect, from_sect = ring("sect")
    vars_, my_var, to_var, from_var = ring("var")
    layers = wqkv.shape[0]
    lat_rows, lon_total, depth = patches.shape
    cols = lon_total // sects
    rows = full.shape[2]
    per = rows // cols
    for layer in range(layers):
        kv_ref[layer, :WL] = jnp.zeros_like(kv_ref[layer, :WL])
        kv_ref[layer, 2 * WL :] = jnp.zeros_like(kv_ref[layer, 2 * WL :])
    q_ref[...] = jnp.zeros_like(q_ref)
    exists = lat_neighbours()
    barrier = pltpu.get_barrier_semaphore()
    my_lat = lax.axis_index("lat")
    for dl in (1, -1):
        @pl.when(exists[dl])
        def _():
            for ds in (0, 1, -1):
                target = {"sect": lax.rem(my_sect + ds + sects, sects), "lat": my_lat + dl}
                pl.semaphore_signal(barrier, inc=1, device_id=target, device_id_type=MESH)
    around = exists[1].astype(jnp.int32) + exists[-1].astype(jnp.int32)
    for axis, size, me in (("sect", sects, my_sect), ("var", vars_, my_var)):
        for d in range(1, size):
            pl.semaphore_signal(
                barrier, inc=1, device_id={axis: lax.rem(me + d, size)}, device_id_type=MESH
            )
    pl.semaphore_wait(barrier, sects + vars_ - 2 + 3 * around)

    last = 4 + 4 * layers
    moved, later = [], []
    for d in range(1, sects):
        t = to_sect[d]
        moved.append(send(table, table_in.at[d - 1], sems, 0, d, "sect", t))
        moved.append(
            send(
                patches.at[:, pl.ds(pl.multiple_of(t * cols, cols), cols), :],
                patch_in.at[d - 1], sems, 1, d, "sect", t,
            )
        )
    params_in[my_var] = params[...]
    for d in range(1, vars_):
        later.append(send(params, params_in.at[my_var], sems, 2, d, "var", to_var[d]))
    for copy in moved:
        copy.wait()
    weights = jnp.concatenate([table[...]] + [table_in[d] for d in range(sects - 1)], axis=0)

    def partial_of(owner):
        lat = pl.ds(owner * per, per)
        own = patches[lat, pl.ds(pl.multiple_of(my_sect * cols, cols), cols), :]
        blocks = [own] + [patch_in[d, lat] for d in range(sects - 1)]
        x = jnp.concatenate([block.reshape(rows, depth) for block in blocks], axis=1)
        return dot(x, weights)

    outgoing = []
    for d in range(1, vars_):
        part[layers, d - 1] = partial_of(to_var[d]).astype(jnp.bfloat16)
        outgoing.append(
            send(part.at[layers, d - 1], part_in.at[layers, d - 1], sems, 3, d, "var", to_var[d])
        )
    total = partial_of(my_var)
    for d in range(1, vars_):
        outgoing[d - 1].wait()
        total = total + part_in[layers, d - 1].astype(jnp.float32)
    full[0, my_var] = total.astype(jnp.bfloat16)
    for d in range(1, sects):
        later.append(send(decode, decode_in.at[d - 1], sems, last, d, "sect", to_sect[d]))
    for layer in range(layers):
        gather_project(
            full.at[layer], wqkv[layer], q_ref, kv_ref.at[layer], sems, 7 + 4 * layer
        )
        if layer == 0:
            for copy in later:
                copy.wait()
        halo(kv_ref.at[layer], halo_send.at[layer], halo_recv.at[layer])
        attention(
            layer, shifts, scales, q_ref, kv_ref.at[layer], wide, q_shifted, kv_shifted,
            framed, attended,
        )
        feed(
            layer, attended, wout, full.at[layer], params_in, w_in, w_out,
            part.at[layer], part_in.at[layer], mid.at[layer], back.at[layer], back_in.at[layer],
            full.at[layer + 1], sems,
        )
    stream = full.at[layers]
    outgoing = [
        send(stream.at[my_var], stream.at[my_var], sems, last + 1, d, "var", to_var[d])
        for d in range(1, vars_)
    ]
    weights = jnp.concatenate([decode[...]] + [decode_in[d] for d in range(sects - 1)], axis=1)
    copies = []
    for k in range(vars_):
        if k:
            outgoing[k - 1].wait()
        lat = pl.ds(from_var[k] * per, per)
        decoded = dot(stream[from_var[k]], weights).astype(jnp.bfloat16)
        for d in range(sects):
            block = decoded[:, d * depth : (d + 1) * depth].reshape(per, cols, depth)
            made[d, lat] = block
            if d:
                copies.append(
                    send(
                        made.at[d, lat], landed.at[sects - d, lat], sems, last + 2 + k, d, "sect",
                        from_sect[d],
                    )
                )
    out_ref[:, pl.ds(pl.multiple_of(my_sect * cols, cols), cols), :] = made[0]
    for copy in copies:
        copy.wait()
    for d in range(1, sects):
        at = pl.ds(pl.multiple_of(to_sect[d] * cols, cols), cols)
        out_ref[:, at, :] = landed[sects - d]


def per_device(
    patches,
    embed_weight,
    qkv_weight,
    out_weight,
    mlp_in_weight,
    mlp_out_weight,
    logit_scale,
    norm_gain,
    norm_bias,
    decode_weight,
    shifts,
):
    _, lat_rows, lon_total, patch_dim = patches.shape
    width = embed_weight.shape[2]
    layers, _, _, head_cols = qkv_weight.shape
    sects, vars_ = lax.axis_size("sect"), lax.axis_size("var")
    cols = lon_total // sects
    tokens = lat_rows * cols
    rows = tokens // vars_
    bf = jnp.bfloat16
    vmem = pl.BlockSpec(memory_space=pltpu.VMEM)
    smem = pl.BlockSpec(memory_space=pltpu.SMEM)
    wqkv = qkv_weight.reshape(layers, width, 3 * head_cols)
    params = jnp.concatenate(
        [norm_gain.reshape(2 * layers, -1), norm_bias.reshape(2 * layers, -1)], axis=0
    )
    shards = pltpu.VMEM((layers + 1, vars_ - 1, rows, width), bf)
    ext_rows, ext_cols = lat_rows + 2 * WL, cols + 2 * WW
    phases = 4 + 4 * layers + 2 + vars_
    scratch = [
        pltpu.VMEM((sects - 1, lat_rows, cols, patch_dim), bf),
        pltpu.VMEM((sects - 1, patch_dim, width), bf),
        pltpu.VMEM((vars_,) + params.shape, jnp.float32),
        shards,
        shards,
        pltpu.VMEM((layers + 1, vars_, rows, width), bf),
        pltpu.VMEM((layers, vars_, rows, width), bf),
        shards,
        shards,
        pltpu.VMEM((ext_rows, ext_cols, head_cols), jnp.float32),
        pltpu.VMEM((layers, ext_rows, ext_cols, 2 * head_cols), bf),
        pltpu.VMEM((ext_rows, ext_cols, 2 * head_cols), jnp.float32),
        pltpu.VMEM((lat_rows + WL, cols + WW, head_cols), bf),
        pltpu.VMEM((lat_rows + WL, cols + WW, 2 * head_cols), bf),
        pltpu.VMEM((lat_rows + WL, cols + WW, head_cols), jnp.float32),
        pltpu.VMEM((tokens, head_cols), bf),
        pltpu.VMEM((sects - 1, width, patch_dim), bf),
        pltpu.VMEM((sects, lat_rows, cols, patch_dim), bf),
        pltpu.VMEM((sects, lat_rows, cols, patch_dim), bf),
        pltpu.SemaphoreType.DMA((phases, 4)),
        pltpu.SemaphoreType.DMA((phases, 4)),
        pltpu.SemaphoreType.DMA((layers, 8)),
        pltpu.SemaphoreType.DMA((layers, 8)),
    ]
    out = pl.pallas_call(
        whole_kernel,
        out_shape=jax.ShapeDtypeStruct((lat_rows, lon_total, patch_dim), bf),
        in_specs=[vmem] * 6 + [smem] + [vmem] * 2 + [smem],
        out_specs=vmem,
        scratch_shapes=scratch,
        compiler_params=pltpu.CompilerParams(
            collective_id=0, has_side_effects=True, vmem_limit_bytes=48 * 1024 * 1024
        ),
    )(
        patches[0], embed_weight[0], wqkv, out_weight, mlp_in_weight, mlp_out_weight,
        logit_scale, params, decode_weight[0], shifts,
    )
    return out[None]


def solution(mesh):
    return jax.shard_map(
        per_device,
        mesh=mesh,
        in_specs=(
            P(("sect", "var"), "lat", None, None),
            P(("sect", "var"), None, None),
            P(None, None, None, "var"),
            P(None, "var", None),
            P(None, None, "var"),
            P(None, "var", None),
            P(None, "var"),
            P(None, None, "var"),
            P(None, None, "var"),
            P(("sect", "var"), None, None),
            P(),
        ),
        out_specs=P(("sect", "var"), "lat", None, None),
        check_vma=False,
    )
```

```python
import jax
import jax.numpy as jnp
from jax import lax
from jax.experimental import pallas as pl
from jax.experimental.pallas import tpu as pltpu
from jax.sharding import PartitionSpec as P

WL = 8
WW = 16
HD = 64
MESH = pl.DeviceIdType.MESH

epsilon = 1e-06


def dot(a, b):
    return jnp.dot(a, b, preferred_element_type=jnp.float32)


def send(src, dst, sems, phase, d, axis, target):
    send_sem, recv_sem = sems
    copy = pltpu.make_async_remote_copy(
        src_ref=src,
        dst_ref=dst,
        send_sem=send_sem.at[phase, d],
        recv_sem=recv_sem.at[phase, d],
        device_id={axis: target},
        device_id_type=MESH,
    )
    copy.start()
    return copy


def ring(axis):
    size = lax.axis_size(axis)
    me = lax.axis_index(axis)
    after = [lax.rem(me + d, size) for d in range(size)]
    before = [lax.rem(me + size - d, size) for d in range(size)]
    return size, me, after, before


def head_unit(x):
    lane = lax.broadcasted_iota(jnp.int32, x.shape, 1)
    square = x * x
    inverse = jnp.zeros_like(x)
    for head in range(x.shape[1] // HD):
        mine = (lane >= head * HD) & (lane < (head + 1) * HD)
        total = jnp.sum(jnp.where(mine, square, 0.0), axis=1, keepdims=True)
        inverse = jnp.where(mine, lax.rsqrt(total + epsilon), inverse)
    return x * inverse


def project_chunk(x, wqkv, q_ref, kv_ref, owner):
    rows, cols = x.shape[0], q_ref.shape[2]
    lon = q_ref.shape[1] - 2 * WW
    per = rows // lon
    projected = dot(x, wqkv)
    lat = pl.ds(WL + owner * per, per)
    inner = slice(WW, WW + lon)
    q_ref[lat, inner, :] = head_unit(projected[:, :cols]).reshape(per, lon, cols)
    keys = head_unit(projected[:, cols : 2 * cols])
    paired = jnp.concatenate([keys, projected[:, 2 * cols :]], axis=1).astype(jnp.bfloat16)
    kv_ref[lat, inner, :] = paired.reshape(per, lon, 2 * cols)


def norm_add(stream, x, gain, bias):
    width = x.shape[1]
    mean = jnp.sum(x, axis=1, keepdims=True) / width
    variance = jnp.sum(x * x, axis=1, keepdims=True) / width - mean * mean
    normed = (x - mean) * lax.rsqrt(variance + 1e-05)
    return (stream.astype(jnp.float32) + gain * normed + bias).astype(jnp.bfloat16)


def gather_project(full, wqkv, q_ref, kv_ref, sems, phase):
    vars_, my_var, to_var, from_var = ring("var")
    outgoing = [
        send(full.at[my_var], full.at[my_var], sems, phase, d, "var", to_var[d])
        for d in range(1, vars_)
    ]
    project_chunk(full[my_var], wqkv, q_ref, kv_ref, my_var)
    for d in range(1, vars_):
        outgoing[d - 1].wait()
        project_chunk(full[from_var[d]], wqkv, q_ref, kv_ref, from_var[d])


def lat_neighbours():
    size, me = lax.axis_size("lat"), lax.axis_index("lat")
    return {1: me < size - 1, -1: me > 0}


def halo(kv_ref, send_sem, recv_sem):
    sects, my_sect = lax.axis_size("sect"), lax.axis_index("sect")
    my_lat = lax.axis_index("lat")
    lon = kv_ref.shape[1] - 2 * WW
    exists = lat_neighbours()
    taken = {0: slice(WW, WW + lon), 1: slice(lon, WW + lon), -1: slice(WW, 2 * WW)}
    placed = {0: slice(WW, WW + lon), 1: slice(0, WW), -1: slice(WW + lon, 2 * WW + lon)}
    landing = {0: slice(WL, 2 * WL), 1: slice(0, WL), -1: slice(2 * WL, 3 * WL)}
    copies = []
    index = 0
    for dl in (1, -1, 0):
        for ds in (0, 1, -1):
            if dl == 0 and ds == 0:
                continue
            target = {"sect": lax.rem(my_sect + ds + sects, sects), "lat": my_lat + dl}
            copy = pltpu.make_async_remote_copy(
                src_ref=kv_ref.at[WL : 2 * WL, taken[ds], :],
                dst_ref=kv_ref.at[landing[dl], placed[ds], :],
                send_sem=send_sem.at[index],
                recv_sem=recv_sem.at[index],
                device_id=target,
                device_id_type=MESH,
            )
            index += 1
            copies.append((dl, copy))
            if dl:
                pl.when(exists[dl])(copy.start)
            else:
                copy.start()
    for dl, copy in copies:
        if dl:
            pl.when(exists[dl])(copy.wait_send)
            pl.when(exists[-dl])(copy.wait_recv)
        else:
            copy.wait()


def attention(layer, shifts, scales, q_ref, kv_ref, wide, q_shifted, kv_shifted, framed, attended):
    lat_rows, lon = WL, q_ref.shape[1] - 2 * WW
    cols = q_ref.shape[2]
    a, b = shifts[layer, 0], shifts[layer, 1]
    my_lat, lats = lax.axis_index("lat"), lax.axis_size("lat")
    wide[...] = kv_ref[...].astype(jnp.float32)
    frame_rows, frame_cols = lat_rows + WL, lon + WW

    def turned(row, step, length):
        return pltpu.roll(row, row.shape[0] - step, 0)[:length].astype(jnp.bfloat16)

    for r in range(frame_rows):
        kv_shifted[r] = turned(wide[a + r], b, frame_cols)
        q_shifted[r] = turned(q_ref[a + r], b, frame_cols)
    lane = lax.broadcasted_iota(jnp.int32, (WL * WW, cols), 1)
    key_row = lax.broadcasted_iota(jnp.int32, (WL * WW, WL * WW), 1) // WW
    heads = cols // HD

    @pl.loop(0, frame_cols // WW)
    def _(n):
        at = pl.ds(pl.multiple_of(n * WW, WW), WW)
        for m in range(frame_rows // WL):
            rows = slice(m * WL, (m + 1) * WL)
            queries = q_shifted[rows, at, :].reshape(WL * WW, cols)
            paired = kv_shifted[rows, at, :].reshape(WL * WW, 2 * cols)
            keys, values = paired[:, :cols], paired[:, cols:]
            place = my_lat * lat_rows - WL + a + m * WL + key_row
            usable = (place >= 0) & (place < lats * lat_rows)
            result = jnp.zeros((WL * WW, cols), jnp.float32)
            for h in range(heads):
                mine = (lane >= h * HD) & (lane < (h + 1) * HD)
                part = jnp.where(mine, queries, jnp.zeros_like(queries))
                scores = lax.dot_general(
                    part, keys, (((1,), (1,)), ((), ())), preferred_element_type=jnp.float32
                )
                scale = scales[layer, h]
                expo = jnp.where(usable, jnp.exp((scores - 1.0) * scale), 0.0)
                total = jnp.sum(expo, axis=1, keepdims=True)
                weights = (expo / total).astype(jnp.bfloat16)
                result = jnp.where(mine, dot(weights, values), result)
            framed[rows, at, :] = result.reshape(WL, WW, cols)

    for r in range(lat_rows):
        attended[r * lon : (r + 1) * lon, :] = turned(framed[WL - a + r], WW - b, lon)


def pieces(stack_rows):
    sect, lat = lax.axis_index("sect"), lax.axis_index("lat")
    core, across, pair = lax.rem(sect, 2), sect // 2, lax.rem(lat, 2)
    step = stack_rows // 8
    own = (core * 2 + across) * 2 + pair
    ranges = [(own, 1), (core * 2 + across, 2), (core, 4)]
    targets = [
        {"lat": lat + 1 - 2 * pair},
        {"sect": sect + 2 - 4 * across},
        {"sect": sect + 1 - 2 * core},
    ]
    at = [
        pl.ds(pl.multiple_of(index * (count * step), 16), count * step) for index, count in ranges
    ]
    return at, targets


def spread(stack, others, send_sem, recv_sem):
    vars_, my_var, to_var, from_var = ring("var")
    at, targets = pieces(stack.shape[0])
    groups = [
        [
            pltpu.make_async_remote_copy(
                src_ref=stack.at[at[0]],
                dst_ref=others.at[d - 1, at[0]],
                send_sem=send_sem.at[d - 1],
                recv_sem=recv_sem.at[d - 1],
                device_id={"var": to_var[d]},
                device_id_type=MESH,
            )
            for d in range(1, vars_)
        ]
    ]
    for k in range(3):
        groups.append(
            [
                pltpu.make_async_remote_copy(
                    src_ref=others.at[:, at[k]],
                    dst_ref=others.at[:, at[k]],
                    send_sem=send_sem.at[vars_ - 1 + k],
                    recv_sem=recv_sem.at[vars_ - 1 + k],
                    device_id=targets[k],
                    device_id_type=MESH,
                )
            ]
        )
    return groups


def advance(groups, stage):
    if stage:
        for copy in groups[stage - 1]:
            copy.wait()
    if stage < len(groups):
        for copy in groups[stage]:
            copy.start()


def feed(layer, attended, attended_in, stack, others, params, x_ref, out_ref, sems, phase):
    vars_, my_var, to_var, from_var = ring("var")
    rows, heads_part = attended_in.shape[1:]
    width = x_ref.shape[2]

    def chosen(kind, position):
        index = (kind * 2 + layer) * 2 + position
        return jnp.concatenate([params[v, index : index + 1, :] for v in range(vars_)], axis=1)

    outgoing = []
    for d in range(1, vars_):
        at = pl.ds(pl.multiple_of(to_var[d] * rows, rows), rows)
        outgoing.append(
            send(attended.at[at], attended_in.at[d - 1], sems, phase, d, "var", to_var[d])
        )
    own = attended[pl.ds(pl.multiple_of(my_var * rows, rows), rows), :]
    total = dot(own, stack[:heads_part])
    for d in range(1, vars_):
        outgoing[d - 1].wait()
        total = total + dot(attended_in[d - 1], others[d - 1, :heads_part])
    mid = norm_add(x_ref[my_var], total, chosen(0, 0), chosen(1, 0))
    first = slice(heads_part, heads_part + width)
    total = jnp.zeros((rows, width), jnp.float32)
    for d in range(vars_):
        shard = stack if d == 0 else others.at[d - 1]
        hidden = jax.nn.gelu(dot(mid, shard[first]), approximate=True).astype(jnp.bfloat16)
        total = total + dot(hidden, shard[heads_part + width :])
    out_ref[my_var] = norm_add(mid, total, chosen(0, 1), chosen(1, 1))


def whole_kernel(
    patches, table, wqkv, stack, scales, params, decode, shifts, out_ref,
    patch_in, table_in, params_in, part, part_in, full, others, attended_in,
    q_ref, kv_ref, wide, q_shifted, kv_shifted, framed, attended,
    decode_in, made, landed, send_sem, recv_sem, halo_send, halo_recv, spread_send, spread_recv,
):
    sems = (send_sem, recv_sem)
    sects, my_sect, to_sect, from_sect = ring("sect")
    vars_, my_var, to_var, from_var = ring("var")
    layers = wqkv.shape[0]
    lat_rows, lon_total, depth = patches.shape
    cols = lon_total // sects
    rows = full.shape[2]
    per = rows // cols
    for layer in range(layers):
        kv_ref[layer, :WL] = jnp.zeros_like(kv_ref[layer, :WL])
        kv_ref[layer, 2 * WL :] = jnp.zeros_like(kv_ref[layer, 2 * WL :])
    q_ref[...] = jnp.zeros_like(q_ref)
    exists = lat_neighbours()
    barrier = pltpu.get_barrier_semaphore()
    my_lat = lax.axis_index("lat")
    for dl in (1, -1):
        @pl.when(exists[dl])
        def _():
            for ds in (0, 1, -1):
                target = {"sect": lax.rem(my_sect + ds + sects, sects), "lat": my_lat + dl}
                pl.semaphore_signal(barrier, inc=1, device_id=target, device_id_type=MESH)
    around = exists[1].astype(jnp.int32) + exists[-1].astype(jnp.int32)
    for axis, size, me in (("sect", sects, my_sect), ("var", vars_, my_var)):
        for d in range(1, size):
            pl.semaphore_signal(
                barrier, inc=1, device_id={axis: lax.rem(me + d, size)}, device_id_type=MESH
            )
    pl.semaphore_wait(barrier, sects + vars_ - 2 + 3 * around)

    last = 4 + 4 * layers
    moved, later = [], []
    for d in range(1, sects):
        t = to_sect[d]
        moved.append(send(table, table_in.at[d - 1], sems, 0, d, "sect", t))
        moved.append(
            send(
                patches.at[:, pl.ds(pl.multiple_of(t * cols, cols), cols), :],
                patch_in.at[d - 1], sems, 1, d, "sect", t,
            )
        )
    params_in[my_var] = params[...]
    for d in range(1, vars_):
        later.append(send(params, params_in.at[my_var], sems, 2, d, "var", to_var[d]))
    carried = [
        spread(stack.at[layer], others.at[layer], spread_send.at[layer], spread_recv.at[layer])
        for layer in range(layers)
    ]
    advance(carried[0], 0)
    for copy in moved:
        copy.wait()
    weights = jnp.concatenate([table[...]] + [table_in[d] for d in range(sects - 1)], axis=0)

    def partial_of(owner):
        lat = pl.ds(owner * per, per)
        own = patches[lat, pl.ds(pl.multiple_of(my_sect * cols, cols), cols), :]
        blocks = [own] + [patch_in[d, lat] for d in range(sects - 1)]
        x = jnp.concatenate([block.reshape(rows, depth) for block in blocks], axis=1)
        return dot(x, weights)

    outgoing = []
    for d in range(1, vars_):
        part[d - 1] = partial_of(to_var[d]).astype(jnp.bfloat16)
        outgoing.append(
            send(part.at[d - 1], part_in.at[d - 1], sems, 3, d, "var", to_var[d])
        )
    advance(carried[0], 1)
    total = partial_of(my_var)
    for d in range(1, vars_):
        outgoing[d - 1].wait()
        total = total + part_in[d - 1].astype(jnp.float32)
    full[0, my_var] = total.astype(jnp.bfloat16)
    for d in range(1, sects):
        later.append(send(decode, decode_in.at[d - 1], sems, last, d, "sect", to_sect[d]))
    advance(carried[0], 2)
    for layer in range(layers):
        gather_project(
            full.at[layer], wqkv[layer], q_ref, kv_ref.at[layer], sems, 7 + 4 * layer
        )
        if layer == 0:
            for copy in later:
                copy.wait()
        advance(carried[layer], 3)
        if layer + 1 < layers:
            advance(carried[layer + 1], 0)
        halo(kv_ref.at[layer], halo_send.at[layer], halo_recv.at[layer])
        attention(
            layer, shifts, scales, q_ref, kv_ref.at[layer], wide, q_shifted, kv_shifted,
            framed, attended.at[layer],
        )
        advance(carried[layer], 4)
        if layer + 1 < layers:
            advance(carried[layer + 1], 1)
        feed(
            layer, attended.at[layer], attended_in.at[layer], stack.at[layer], others.at[layer],
            params_in, full.at[layer], full.at[layer + 1], sems, 4 + 4 * layer,
        )
        if layer + 1 < layers:
            advance(carried[layer + 1], 2)
    stream = full.at[layers]
    outgoing = [
        send(stream.at[my_var], stream.at[my_var], sems, last + 1, d, "var", to_var[d])
        for d in range(1, vars_)
    ]
    weights = jnp.concatenate([decode[...]] + [decode_in[d] for d in range(sects - 1)], axis=1)
    copies = []
    for k in range(vars_):
        if k:
            outgoing[k - 1].wait()
        lat = pl.ds(from_var[k] * per, per)
        decoded = dot(stream[from_var[k]], weights).astype(jnp.bfloat16)
        for d in range(sects):
            block = decoded[:, d * depth : (d + 1) * depth].reshape(per, cols, depth)
            made[d, lat] = block
            if d:
                copies.append(
                    send(
                        made.at[d, lat], landed.at[sects - d, lat], sems, last + 2 + k, d, "sect",
                        from_sect[d],
                    )
                )
    out_ref[:, pl.ds(pl.multiple_of(my_sect * cols, cols), cols), :] = made[0]
    for copy in copies:
        copy.wait()
    for d in range(1, sects):
        at = pl.ds(pl.multiple_of(to_sect[d] * cols, cols), cols)
        out_ref[:, at, :] = landed[sects - d]


def per_device(
    patches,
    embed_weight,
    qkv_weight,
    out_weight,
    mlp_in_weight,
    mlp_out_weight,
    logit_scale,
    norm_gain,
    norm_bias,
    decode_weight,
    shifts,
):
    _, lat_rows, lon_total, patch_dim = patches.shape
    width = embed_weight.shape[2]
    layers, _, _, head_cols = qkv_weight.shape
    sects, vars_ = lax.axis_size("sect"), lax.axis_size("var")
    cols = lon_total // sects
    tokens = lat_rows * cols
    rows = tokens // vars_
    bf = jnp.bfloat16
    vmem = pl.BlockSpec(memory_space=pltpu.VMEM)
    smem = pl.BlockSpec(memory_space=pltpu.SMEM)
    wqkv = qkv_weight.reshape(layers, width, 3 * head_cols)
    params = jnp.concatenate(
        [norm_gain.reshape(2 * layers, -1), norm_bias.reshape(2 * layers, -1)], axis=0
    )
    stack = jnp.concatenate([out_weight, mlp_in_weight, mlp_out_weight], axis=1)
    shards = pltpu.VMEM((vars_ - 1, rows, width), bf)
    ext_rows, ext_cols = lat_rows + 2 * WL, cols + 2 * WW
    phases = 4 + 4 * layers + 2 + vars_
    scratch = [
        pltpu.VMEM((sects - 1, lat_rows, cols, patch_dim), bf),
        pltpu.VMEM((sects - 1, patch_dim, width), bf),
        pltpu.VMEM((vars_,) + params.shape, jnp.float32),
        shards,
        shards,
        pltpu.VMEM((layers + 1, vars_, rows, width), bf),
        pltpu.VMEM((layers, vars_ - 1) + stack.shape[1:], bf),
        pltpu.VMEM((layers, vars_ - 1, rows, head_cols), bf),
        pltpu.VMEM((ext_rows, ext_cols, head_cols), jnp.float32),
        pltpu.VMEM((layers, ext_rows, ext_cols, 2 * head_cols), bf),
        pltpu.VMEM((ext_rows, ext_cols, 2 * head_cols), jnp.float32),
        pltpu.VMEM((lat_rows + WL, cols + WW, head_cols), bf),
        pltpu.VMEM((lat_rows + WL, cols + WW, 2 * head_cols), bf),
        pltpu.VMEM((lat_rows + WL, cols + WW, head_cols), jnp.float32),
        pltpu.VMEM((layers, tokens, head_cols), bf),
        pltpu.VMEM((sects - 1, width, patch_dim), bf),
        pltpu.VMEM((sects, lat_rows, cols, patch_dim), bf),
        pltpu.VMEM((sects, lat_rows, cols, patch_dim), bf),
        pltpu.SemaphoreType.DMA((phases, 4)),
        pltpu.SemaphoreType.DMA((phases, 4)),
        pltpu.SemaphoreType.DMA((layers, 8)),
        pltpu.SemaphoreType.DMA((layers, 8)),
        pltpu.SemaphoreType.DMA((layers, vars_ + 2)),
        pltpu.SemaphoreType.DMA((layers, vars_ + 2)),
    ]
    out = pl.pallas_call(
        whole_kernel,
        out_shape=jax.ShapeDtypeStruct((lat_rows, lon_total, patch_dim), bf),
        in_specs=[vmem] * 4 + [smem] + [vmem] * 2 + [smem],
        out_specs=vmem,
        scratch_shapes=scratch,
        compiler_params=pltpu.CompilerParams(
            collective_id=0, has_side_effects=True, vmem_limit_bytes=48 * 1024 * 1024
        ),
    )(
        patches[0], embed_weight[0], wqkv, stack,
        logit_scale, params, decode_weight[0], shifts,
    )
    return out[None]


def solution(mesh):
    return jax.shard_map(
        per_device,
        mesh=mesh,
        in_specs=(
            P(("sect", "var"), "lat", None, None),
            P(("sect", "var"), None, None),
            P(None, None, None, "var"),
            P(None, "var", None),
            P(None, None, "var"),
            P(None, "var", None),
            P(None, "var"),
            P(None, None, "var"),
            P(None, None, "var"),
            P(("sect", "var"), None, None),
            P(),
        ),
        out_specs=P(("sect", "var"), "lat", None, None),
        check_vma=False,
    )
```

```python
import jax
import jax.numpy as jnp
from jax import lax
from jax.experimental import pallas as pl
from jax.experimental.pallas import tpu as pltpu
from jax.sharding import PartitionSpec as P

WL = 8
WW = 16
HD = 64
MESH = pl.DeviceIdType.MESH

epsilon = 1e-06


def dot(a, b):
    return jnp.dot(a, b, preferred_element_type=jnp.float32)


def send(src, dst, sems, phase, d, axis, target):
    send_sem, recv_sem = sems
    copy = pltpu.make_async_remote_copy(
        src_ref=src,
        dst_ref=dst,
        send_sem=send_sem.at[phase, d],
        recv_sem=recv_sem.at[phase, d],
        device_id={axis: target},
        device_id_type=MESH,
    )
    copy.start()
    return copy


def ring(axis):
    size = lax.axis_size(axis)
    me = lax.axis_index(axis)
    after = [lax.rem(me + d, size) for d in range(size)]
    before = [lax.rem(me + size - d, size) for d in range(size)]
    return size, me, after, before


def head_unit(x):
    lane = lax.broadcasted_iota(jnp.int32, x.shape, 1)
    square = x * x
    inverse = jnp.zeros_like(x)
    for head in range(x.shape[1] // HD):
        mine = (lane >= head * HD) & (lane < (head + 1) * HD)
        total = jnp.sum(jnp.where(mine, square, 0.0), axis=1, keepdims=True)
        inverse = jnp.where(mine, lax.rsqrt(total + epsilon), inverse)
    return x * inverse


def project_chunk(x, wqkv, q_ref, kv_ref, owner):
    rows, cols = x.shape[0], q_ref.shape[2]
    lon = q_ref.shape[1] - 2 * WW
    per = rows // lon
    projected = dot(x, jnp.concatenate([wqkv[i] for i in range(3)], axis=1))
    lat = pl.ds(WL + owner * per, per)
    inner = slice(WW, WW + lon)
    q_ref[lat, inner, :] = head_unit(projected[:, :cols]).reshape(per, lon, cols)
    keys = head_unit(projected[:, cols : 2 * cols])
    paired = jnp.concatenate([keys, projected[:, 2 * cols :]], axis=1).astype(jnp.bfloat16)
    kv_ref[lat, inner, :] = paired.reshape(per, lon, 2 * cols)


def norm_add(stream, x, gain, bias):
    width = x.shape[1]
    mean = jnp.sum(x, axis=1, keepdims=True) / width
    variance = jnp.sum(x * x, axis=1, keepdims=True) / width - mean * mean
    normed = (x - mean) * lax.rsqrt(variance + 1e-05)
    return (stream.astype(jnp.float32) + gain * normed + bias).astype(jnp.bfloat16)


def gather_project(full, wqkv, q_ref, kv_ref, sems, phase, halo_sems):
    vars_, my_var, to_var, from_var = ring("var")
    outgoing = [
        send(full.at[my_var], full.at[my_var], sems, phase, d, "var", to_var[d])
        for d in range(1, vars_)
    ]
    per = full.shape[1] // (kv_ref.shape[1] - 2 * WW)
    copies = []
    for d in range(vars_):
        if d:
            outgoing[d - 1].wait()
        project_chunk(full[from_var[d]], wqkv, q_ref, kv_ref, from_var[d])
        copies += halo(kv_ref, from_var[d] * per, per, halo_sems, d)
    exists = lat_neighbours()
    for dl, copy in copies:
        if dl:
            pl.when(exists[dl])(copy.wait_send)
            pl.when(exists[-dl])(copy.wait_recv)
        else:
            copy.wait()


def lat_neighbours():
    size, me = lax.axis_size("lat"), lax.axis_index("lat")
    return {1: me < size - 1, -1: me > 0}


def halo(kv_ref, start, per, halo_sems, chunk):
    sects, my_sect = lax.axis_size("sect"), lax.axis_index("sect")
    my_lat = lax.axis_index("lat")
    lon = kv_ref.shape[1] - 2 * WW
    exists = lat_neighbours()
    taken = {0: slice(WW, WW + lon), 1: slice(lon, WW + lon), -1: slice(WW, 2 * WW)}
    placed = {0: slice(WW, WW + lon), 1: slice(0, WW), -1: slice(WW + lon, 2 * WW + lon)}
    landing = {0: WL, 1: 0, -1: 2 * WL}
    send_sem, recv_sem = halo_sems
    copies = []
    index = 0
    for dl in (1, -1, 0):
        for ds in (0, 1, -1):
            if dl == 0 and ds == 0:
                continue
            target = {"sect": lax.rem(my_sect + ds + sects, sects), "lat": my_lat + dl}
            copy = pltpu.make_async_remote_copy(
                src_ref=kv_ref.at[pl.ds(WL + start, per), taken[ds], :],
                dst_ref=kv_ref.at[pl.ds(landing[dl] + start, per), placed[ds], :],
                send_sem=send_sem.at[chunk, index],
                recv_sem=recv_sem.at[chunk, index],
                device_id=target,
                device_id_type=MESH,
            )
            index += 1
            copies.append((dl, copy))
            if dl:
                pl.when(exists[dl])(copy.start)
            else:
                copy.start()
    return copies


def attention(layer, shifts, scales, q_ref, kv_ref, wide, q_shifted, kv_shifted, framed, attended):
    lat_rows, lon = WL, q_ref.shape[1] - 2 * WW
    cols = q_ref.shape[2]
    a, b = shifts[layer, 0], shifts[layer, 1]
    my_lat, lats = lax.axis_index("lat"), lax.axis_size("lat")
    wide[...] = kv_ref[...].astype(jnp.float32)
    frame_rows, frame_cols = lat_rows + WL, lon + WW

    def turned(row, step, length):
        return pltpu.roll(row, row.shape[0] - step, 0)[:length].astype(jnp.bfloat16)

    for r in range(frame_rows):
        kv_shifted[r] = turned(wide[a + r], b, frame_cols)
        q_shifted[r] = turned(q_ref[a + r], b, frame_cols)
    lane = lax.broadcasted_iota(jnp.int32, (WL * WW, cols), 1)
    key_row = lax.broadcasted_iota(jnp.int32, (WL * WW, WL * WW), 1) // WW
    heads = cols // HD

    for n in range(frame_cols // WW):
        at = slice(n * WW, (n + 1) * WW)
        for m in range(frame_rows // WL):
            rows = slice(m * WL, (m + 1) * WL)
            queries = q_shifted[rows, at, :].reshape(WL * WW, cols)
            paired = kv_shifted[rows, at, :].reshape(WL * WW, 2 * cols)
            keys, values = paired[:, :cols], paired[:, cols:]
            place = my_lat * lat_rows - WL + a + m * WL + key_row
            usable = (place >= 0) & (place < lats * lat_rows)
            result = jnp.zeros((WL * WW, cols), jnp.float32)
            for h in range(heads):
                mine = (lane >= h * HD) & (lane < (h + 1) * HD)
                part = jnp.where(mine, queries, jnp.zeros_like(queries))
                scores = lax.dot_general(
                    part, keys, (((1,), (1,)), ((), ())), preferred_element_type=jnp.float32
                )
                scale = scales[layer, h]
                expo = jnp.where(usable, jnp.exp((scores - 1.0) * scale), 0.0)
                total = jnp.sum(expo, axis=1, keepdims=True)
                mixed = dot(expo.astype(jnp.bfloat16), values) * (1.0 / total)
                result = jnp.where(mine, mixed, result)
            framed[rows, at, :] = result.reshape(WL, WW, cols)

    for r in range(lat_rows):
        attended[r * lon : (r + 1) * lon, :] = turned(framed[WL - a + r], WW - b, lon)


def pieces(stack_rows, lat_first):
    sect, lat = lax.axis_index("sect"), lax.axis_index("lat")
    core, across, pair = lax.rem(sect, 2), sect // 2, lax.rem(lat, 2)
    step = stack_rows // 8
    by_lat, by_chip = {"lat": lat + 1 - 2 * pair}, {"sect": sect + 2 - 4 * across}
    by_core = {"sect": sect + 1 - 2 * core}
    if lat_first:
        outer, inner, targets = across, pair, [by_lat, by_chip, by_core]
    else:
        outer, inner, targets = pair, across, [by_chip, by_lat, by_core]
    ranges = [((core * 2 + outer) * 2 + inner, 1), (core * 2 + outer, 2), (core, 4)]
    at = [
        pl.ds(pl.multiple_of(index * (count * step), 16), count * step) for index, count in ranges
    ]
    return at, targets


def spread(stack, others, send_sem, recv_sem, lat_first):
    vars_, my_var, to_var, from_var = ring("var")
    at, targets = pieces(stack.shape[0], lat_first)
    groups = [
        [
            pltpu.make_async_remote_copy(
                src_ref=stack.at[at[0]],
                dst_ref=others.at[d - 1, at[0]],
                send_sem=send_sem.at[d - 1],
                recv_sem=recv_sem.at[d - 1],
                device_id={"var": to_var[d]},
                device_id_type=MESH,
            )
            for d in range(1, vars_)
        ]
    ]
    for k in range(3):
        groups.append(
            [
                pltpu.make_async_remote_copy(
                    src_ref=others.at[:, at[k]],
                    dst_ref=others.at[:, at[k]],
                    send_sem=send_sem.at[vars_ - 1 + k],
                    recv_sem=recv_sem.at[vars_ - 1 + k],
                    device_id=targets[k],
                    device_id_type=MESH,
                )
            ]
        )
    return groups


def advance(groups, stage):
    if stage:
        for copy in groups[stage - 1]:
            copy.wait()
    if stage < len(groups):
        for copy in groups[stage]:
            copy.start()


def feed(layer, attended, attended_in, stack, others, params, x_ref, out_ref, sems, phase):
    vars_, my_var, to_var, from_var = ring("var")
    rows, heads_part = attended_in.shape[1:]
    width = x_ref.shape[2]

    def chosen(kind, position):
        index = (kind * 2 + layer) * 2 + position
        return jnp.concatenate([params[v, index : index + 1, :] for v in range(vars_)], axis=1)

    outgoing = []
    for d in range(1, vars_):
        at = pl.ds(pl.multiple_of(to_var[d] * rows, rows), rows)
        outgoing.append(
            send(attended.at[at], attended_in.at[d - 1], sems, phase, d, "var", to_var[d])
        )
    own = attended[pl.ds(pl.multiple_of(my_var * rows, rows), rows), :]
    total = dot(own, stack[:heads_part])
    for d in range(1, vars_):
        outgoing[d - 1].wait()
        total = total + dot(attended_in[d - 1], others[d - 1, :heads_part])
    mid = norm_add(x_ref[my_var], total, chosen(0, 0), chosen(1, 0))
    first = slice(heads_part, heads_part + width)
    total = jnp.zeros((rows, width), jnp.float32)
    for d in range(vars_):
        shard = stack if d == 0 else others.at[d - 1]
        hidden = jax.nn.gelu(dot(mid, shard[first]), approximate=True).astype(jnp.bfloat16)
        total = total + dot(hidden, shard[heads_part + width :])
    out_ref[my_var] = norm_add(mid, total, chosen(0, 1), chosen(1, 1))


def whole_kernel(
    patches, table, wqkv, wout, w_in, w_out, scales, gains, biases, decode, shifts, out_ref,
    stack, patch_in, table_in, params_in, part, part_in, full, others, attended_in,
    q_ref, kv_ref, wide, q_shifted, kv_shifted, framed, attended,
    decode_in, made, landed, send_sem, recv_sem, halo_send, halo_recv, spread_send, spread_recv, patch_send, patch_recv,
):
    sems = (send_sem, recv_sem)
    sects, my_sect, to_sect, from_sect = ring("sect")
    vars_, my_var, to_var, from_var = ring("var")
    layers = wqkv.shape[0]
    lat_rows, lon_total, depth = patches.shape
    cols = lon_total // sects
    rows = full.shape[2]
    per = rows // cols
    for layer in range(layers):
        kv_ref[layer, :WL] = jnp.zeros_like(kv_ref[layer, :WL])
        kv_ref[layer, 2 * WL :] = jnp.zeros_like(kv_ref[layer, 2 * WL :])
    q_ref[...] = jnp.zeros_like(q_ref)
    at = 0
    for weight in (wout, w_in, w_out):
        stack[:, at : at + weight.shape[1], :] = weight[...]
        at += weight.shape[1]
    exists = lat_neighbours()
    barrier = pltpu.get_barrier_semaphore()
    my_lat = lax.axis_index("lat")
    for dl in (1, -1):
        @pl.when(exists[dl])
        def _():
            for ds in (0, 1, -1):
                target = {"sect": lax.rem(my_sect + ds + sects, sects), "lat": my_lat + dl}
                pl.semaphore_signal(barrier, inc=1, device_id=target, device_id_type=MESH)
    around = exists[1].astype(jnp.int32) + exists[-1].astype(jnp.int32)
    for axis, size, me in (("sect", sects, my_sect), ("var", vars_, my_var)):
        for d in range(1, size):
            pl.semaphore_signal(
                barrier, inc=1, device_id={axis: lax.rem(me + d, size)}, device_id_type=MESH
            )
    pl.semaphore_wait(barrier, sects + vars_ - 2 + 3 * around)

    last = 4 + 4 * layers
    later = []
    other_core = my_sect + 1 - 2 * lax.rem(my_sect, 2)
    other_chip = lax.rem(my_sect + 2, sects)

    def pass_table(source, owner, target, index):
        slot = lax.rem(target - owner + sects, sects) - 1
        return send(source, table_in.at[slot], sems, 0, index, "sect", target)

    tables = [pass_table(table, my_sect, other_chip, 0), pass_table(table, my_sect, other_core, 1)]
    chunks = []
    for k in range(vars_):
        lat = pl.ds(to_var[(k + 1) % vars_] * per, per)
        group = []
        for d in range(1, sects):
            at = pl.ds(pl.multiple_of(to_sect[d] * cols, cols), cols)
            copy = pltpu.make_async_remote_copy(
                src_ref=patches.at[lat, at, :],
                dst_ref=patch_in.at[d - 1, lat],
                send_sem=patch_send.at[k, d],
                recv_sem=patch_recv.at[k, d],
                device_id={"sect": to_sect[d]},
                device_id_type=MESH,
            )
            copy.start()
            group.append(copy)
        chunks.append(group)
    lines = gains.shape[0]
    params_in[my_var, :lines] = gains[...]
    params_in[my_var, lines:] = biases[...]
    for d in range(1, vars_):
        own = params_in.at[my_var]
        later.append(send(own, own, sems, 2, d, "var", to_var[d]))
    stack_rows = stack.shape[1]
    half = (stack_rows // 128 + 1) // 2 * 128
    carried = []
    for layer in range(layers):
        halves = [
            spread(
                stack.at[layer, at], others.at[layer, :, at],
                spread_send.at[layer, k], spread_recv.at[layer, k], k == 0,
            )
            for k, at in enumerate((slice(0, half), slice(half, stack_rows)))
        ]
        carried.append([a + b for a, b in zip(*halves)])
    advance(carried[0], 0)
    tables[0].wait()
    relayed = pass_table(table_in.at[sects // 2 - 1], other_chip, other_core, 2)
    tables[1].wait()
    relayed.wait()
    weights = jnp.concatenate([table[...]] + [table_in[d] for d in range(sects - 1)], axis=0)

    def partial_of(owner):
        lat = pl.ds(owner * per, per)
        own = patches[lat, pl.ds(pl.multiple_of(my_sect * cols, cols), cols), :]
        blocks = [own] + [patch_in[d, lat] for d in range(sects - 1)]
        x = jnp.concatenate([block.reshape(rows, depth) for block in blocks], axis=1)
        return dot(x, weights)

    outgoing = []
    for d in range(1, vars_):
        for copy in chunks[d - 1]:
            copy.wait()
        part[d - 1] = partial_of(to_var[d]).astype(jnp.bfloat16)
        outgoing.append(
            send(part.at[d - 1], part_in.at[d - 1], sems, 3, d, "var", to_var[d])
        )
    advance(carried[0], 1)
    for copy in chunks[vars_ - 1]:
        copy.wait()
    total = partial_of(my_var)
    for d in range(1, vars_):
        outgoing[d - 1].wait()
        total = total + part_in[d - 1].astype(jnp.float32)
    full[0, my_var] = total.astype(jnp.bfloat16)
    for d in range(1, sects):
        later.append(send(decode, decode_in.at[d - 1], sems, last, d, "sect", to_sect[d]))
    advance(carried[0], 2)
    for layer in range(layers):
        gather_project(
            full.at[layer], wqkv.at[layer], q_ref, kv_ref.at[layer], sems, 7 + 4 * layer,
            (halo_send.at[layer], halo_recv.at[layer]),
        )
        if layer == 0:
            for copy in later:
                copy.wait()
        advance(carried[layer], 3)
        if layer + 1 < layers:
            advance(carried[layer + 1], 0)
        attention(
            layer, shifts, scales, q_ref, kv_ref.at[layer], wide, q_shifted, kv_shifted,
            framed, attended.at[layer],
        )
        advance(carried[layer], 4)
        if layer + 1 < layers:
            advance(carried[layer + 1], 1)
        feed(
            layer, attended.at[layer], attended_in.at[layer], stack.at[layer], others.at[layer],
            params_in, full.at[layer], full.at[layer + 1], sems, 4 + 4 * layer,
        )
        if layer + 1 < layers:
            advance(carried[layer + 1], 2)
    stream = full.at[layers]
    outgoing = [
        send(stream.at[my_var], stream.at[my_var], sems, last + 1, d, "var", to_var[d])
        for d in range(1, vars_)
    ]
    weights = jnp.concatenate([decode[...]] + [decode_in[d] for d in range(sects - 1)], axis=1)
    copies = []
    for k in range(vars_):
        if k:
            outgoing[k - 1].wait()
        lat = pl.ds(from_var[k] * per, per)
        decoded = dot(stream[from_var[k]], weights).astype(jnp.bfloat16)
        for d in range(sects):
            block = decoded[:, d * depth : (d + 1) * depth].reshape(per, cols, depth)
            made[d, lat] = block
            if d:
                copies.append(
                    send(
                        made.at[d, lat], landed.at[sects - d, lat], sems, last + 2 + k, d, "sect",
                        from_sect[d],
                    )
                )
    out_ref[:, pl.ds(pl.multiple_of(my_sect * cols, cols), cols), :] = made[0]
    for copy in copies:
        copy.wait()
    for d in range(1, sects):
        at = pl.ds(pl.multiple_of(to_sect[d] * cols, cols), cols)
        out_ref[:, at, :] = landed[sects - d]


def per_device(
    patches,
    embed_weight,
    qkv_weight,
    out_weight,
    mlp_in_weight,
    mlp_out_weight,
    logit_scale,
    norm_gain,
    norm_bias,
    decode_weight,
    shifts,
):
    _, lat_rows, lon_total, patch_dim = patches.shape
    width = embed_weight.shape[2]
    layers, _, _, head_cols = qkv_weight.shape
    sects, vars_ = lax.axis_size("sect"), lax.axis_size("var")
    cols = lon_total // sects
    tokens = lat_rows * cols
    rows = tokens // vars_
    bf = jnp.bfloat16
    vmem = pl.BlockSpec(memory_space=pltpu.VMEM)
    smem = pl.BlockSpec(memory_space=pltpu.SMEM)
    wqkv = qkv_weight.transpose(0, 2, 1, 3)
    gains, biases = norm_gain.reshape(2 * layers, -1), norm_bias.reshape(2 * layers, -1)
    stack_rows = out_weight.shape[1] + mlp_in_weight.shape[1] + mlp_out_weight.shape[1]
    shards = pltpu.VMEM((vars_ - 1, rows, width), bf)
    ext_rows, ext_cols = lat_rows + 2 * WL, cols + 2 * WW
    phases = 4 + 4 * layers + 2 + vars_
    scratch = [
        pltpu.VMEM((layers, stack_rows, width), bf),
        pltpu.VMEM((sects - 1, lat_rows, cols, patch_dim), bf),
        pltpu.VMEM((sects - 1, patch_dim, width), bf),
        pltpu.VMEM((vars_, 4 * layers, gains.shape[1]), jnp.float32),
        shards,
        shards,
        pltpu.VMEM((layers + 1, vars_, rows, width), bf),
        pltpu.VMEM((layers, vars_ - 1, stack_rows, width), bf),
        pltpu.VMEM((layers, vars_ - 1, rows, head_cols), bf),
        pltpu.VMEM((ext_rows, ext_cols, head_cols), jnp.float32),
        pltpu.VMEM((layers, ext_rows, ext_cols, 2 * head_cols), bf),
        pltpu.VMEM((ext_rows, ext_cols, 2 * head_cols), jnp.float32),
        pltpu.VMEM((lat_rows + WL, cols + WW, head_cols), bf),
        pltpu.VMEM((lat_rows + WL, cols + WW, 2 * head_cols), bf),
        pltpu.VMEM((lat_rows + WL, cols + WW, head_cols), jnp.float32),
        pltpu.VMEM((layers, tokens, head_cols), bf),
        pltpu.VMEM((sects - 1, width, patch_dim), bf),
        pltpu.VMEM((sects, lat_rows, cols, patch_dim), bf),
        pltpu.VMEM((sects, lat_rows, cols, patch_dim), bf),
        pltpu.SemaphoreType.DMA((phases, 4)),
        pltpu.SemaphoreType.DMA((phases, 4)),
        pltpu.SemaphoreType.DMA((layers, vars_, 8)),
        pltpu.SemaphoreType.DMA((layers, vars_, 8)),
        pltpu.SemaphoreType.DMA((layers, 2, vars_ + 2)),
        pltpu.SemaphoreType.DMA((layers, 2, vars_ + 2)),
        pltpu.SemaphoreType.DMA((vars_, sects)),
        pltpu.SemaphoreType.DMA((vars_, sects)),
    ]
    out = pl.pallas_call(
        whole_kernel,
        out_shape=jax.ShapeDtypeStruct((lat_rows, lon_total, patch_dim), bf),
        in_specs=[vmem] * 6 + [smem] + [vmem] * 3 + [smem],
        out_specs=vmem,
        scratch_shapes=scratch,
        compiler_params=pltpu.CompilerParams(
            collective_id=0, has_side_effects=True, vmem_limit_bytes=48 * 1024 * 1024
        ),
    )(
        patches[0], embed_weight[0], wqkv, out_weight, mlp_in_weight, mlp_out_weight,
        logit_scale, gains, biases, decode_weight[0], shifts,
    )
    return out[None]


def solution(mesh):
    return jax.shard_map(
        per_device,
        mesh=mesh,
        in_specs=(
            P(("sect", "var"), "lat", None, None),
            P(("sect", "var"), None, None),
            P(None, None, None, "var"),
            P(None, "var", None),
            P(None, None, "var"),
            P(None, "var", None),
            P(None, "var"),
            P(None, None, "var"),
            P(None, None, "var"),
            P(("sect", "var"), None, None),
            P(),
        ),
        out_specs=P(("sect", "var"), "lat", None, None),
        check_vma=False,
    )
```

```python
import jax
import jax.numpy as jnp
from jax import lax
from jax.experimental import pallas as pl
from jax.experimental.pallas import tpu as pltpu
from jax.sharding import PartitionSpec as P

WL = 8
WW = 16
HD = 64
MESH = pl.DeviceIdType.MESH

epsilon = 1e-06


def dot(a, b):
    return jnp.dot(a, b, preferred_element_type=jnp.float32)


def send(src, dst, sems, phase, d, axis, target):
    send_sem, recv_sem = sems
    copy = pltpu.make_async_remote_copy(
        src_ref=src,
        dst_ref=dst,
        send_sem=send_sem.at[phase, d],
        recv_sem=recv_sem.at[phase, d],
        device_id={axis: target},
        device_id_type=MESH,
    )
    copy.start()
    return copy


def ring(axis):
    size = lax.axis_size(axis)
    me = lax.axis_index(axis)
    after = [lax.rem(me + d, size) for d in range(size)]
    before = [lax.rem(me + size - d, size) for d in range(size)]
    return size, me, after, before


def head_unit(x):
    lane = lax.broadcasted_iota(jnp.int32, x.shape, 1)
    square = x * x
    inverse = jnp.zeros_like(x)
    for head in range(x.shape[1] // HD):
        mine = (lane >= head * HD) & (lane < (head + 1) * HD)
        total = jnp.sum(jnp.where(mine, square, 0.0), axis=1, keepdims=True)
        inverse = jnp.where(mine, lax.rsqrt(total + epsilon), inverse)
    return x * inverse


def project_chunk(x, wqkv, q_ref, kv_ref, owner):
    rows, cols = x.shape[0], q_ref.shape[2]
    lon = q_ref.shape[1] - 2 * WW
    per = rows // lon
    projected = dot(x, jnp.concatenate([wqkv[i] for i in range(3)], axis=1))
    lat = pl.ds(WL + owner * per, per)
    inner = slice(WW, WW + lon)
    q_ref[lat, inner, :] = head_unit(projected[:, :cols]).reshape(per, lon, cols)
    keys = head_unit(projected[:, cols : 2 * cols])
    paired = jnp.concatenate([keys, projected[:, 2 * cols :]], axis=1).astype(jnp.bfloat16)
    kv_ref[lat, inner, :] = paired.reshape(per, lon, 2 * cols)


def norm_add(stream, x, gain, bias):
    width = x.shape[1]
    mean = jnp.sum(x, axis=1, keepdims=True) / width
    variance = jnp.sum(x * x, axis=1, keepdims=True) / width - mean * mean
    normed = (x - mean) * lax.rsqrt(variance + 1e-05)
    return (stream.astype(jnp.float32) + gain * normed + bias).astype(jnp.bfloat16)


def gather_project(full, wqkv, q_ref, kv_ref, sems, phase, halo_sems):
    vars_, my_var, to_var, from_var = ring("var")
    outgoing = [
        send(full.at[my_var], full.at[my_var], sems, phase, d, "var", to_var[d])
        for d in range(1, vars_)
    ]
    per = full.shape[1] // (kv_ref.shape[1] - 2 * WW)
    copies = []
    for d in range(vars_):
        if d:
            outgoing[d - 1].wait()
        project_chunk(full[from_var[d]], wqkv, q_ref, kv_ref, from_var[d])
        copies += halo(kv_ref, from_var[d] * per, per, halo_sems, d)
    exists = lat_neighbours()
    for dl, copy in copies:
        if dl:
            pl.when(exists[dl])(copy.wait_send)
            pl.when(exists[-dl])(copy.wait_recv)
        else:
            copy.wait()


def lat_neighbours():
    size, me = lax.axis_size("lat"), lax.axis_index("lat")
    return {1: me < size - 1, -1: me > 0}


def halo(kv_ref, start, per, halo_sems, chunk):
    sects, my_sect = lax.axis_size("sect"), lax.axis_index("sect")
    my_lat = lax.axis_index("lat")
    lon = kv_ref.shape[1] - 2 * WW
    exists = lat_neighbours()
    taken = {0: slice(WW, WW + lon), 1: slice(lon, WW + lon), -1: slice(WW, 2 * WW)}
    placed = {0: slice(WW, WW + lon), 1: slice(0, WW), -1: slice(WW + lon, 2 * WW + lon)}
    landing = {0: WL, 1: 0, -1: 2 * WL}
    send_sem, recv_sem = halo_sems
    copies = []
    index = 0
    for dl in (1, -1, 0):
        for ds in (0, 1, -1):
            if dl == 0 and ds == 0:
                continue
            target = {"sect": lax.rem(my_sect + ds + sects, sects), "lat": my_lat + dl}
            copy = pltpu.make_async_remote_copy(
                src_ref=kv_ref.at[pl.ds(WL + start, per), taken[ds], :],
                dst_ref=kv_ref.at[pl.ds(landing[dl] + start, per), placed[ds], :],
                send_sem=send_sem.at[chunk, index],
                recv_sem=recv_sem.at[chunk, index],
                device_id=target,
                device_id_type=MESH,
            )
            index += 1
            copies.append((dl, copy))
            if dl:
                pl.when(exists[dl])(copy.start)
            else:
                copy.start()
    return copies


def attention(
    layer, shifts, scales, q_ref, kv_ref, wide, q_shifted, kv_shifted, framed, attended, between
):
    lat_rows, lon = WL, q_ref.shape[1] - 2 * WW
    cols = q_ref.shape[2]
    a, b = shifts[layer, 0], shifts[layer, 1]
    my_lat, lats = lax.axis_index("lat"), lax.axis_size("lat")
    wide[...] = kv_ref[...].astype(jnp.float32)
    frame_rows, frame_cols = lat_rows + WL, lon + WW

    def turned(row, step, length):
        return pltpu.roll(row, row.shape[0] - step, 0)[:length].astype(jnp.bfloat16)

    for r in range(frame_rows):
        kv_shifted[r] = turned(wide[a + r], b, frame_cols)
        q_shifted[r] = turned(q_ref[a + r], b, frame_cols)
    heads, window = cols // HD, WL * WW
    lane = lax.broadcasted_iota(jnp.int32, (window, cols), 1)
    key_row = lax.broadcasted_iota(jnp.int32, (heads * window, window), 1) // WW
    head_row = lax.broadcasted_iota(jnp.int32, (heads * window, window), 0) // window
    scale = jnp.zeros((heads * window, window), jnp.float32)
    for h in range(heads):
        scale = jnp.where(head_row == h, scales[layer, h], scale)
    masks = [(lane >= h * HD) & (lane < (h + 1) * HD) for h in range(heads)]

    for n in range(frame_cols // WW):
        at = slice(n * WW, (n + 1) * WW)
        for m in range(frame_rows // WL):
            rows = slice(m * WL, (m + 1) * WL)
            queries = q_shifted[rows, at, :].reshape(window, cols)
            paired = kv_shifted[rows, at, :].reshape(window, 2 * cols)
            keys, values = paired[:, :cols], paired[:, cols:]
            place = my_lat * lat_rows - WL + a + m * WL + key_row
            usable = (place >= 0) & (place < lats * lat_rows)
            split = jnp.concatenate(
                [jnp.where(mine, queries, jnp.zeros_like(queries)) for mine in masks], axis=0
            )
            scores = lax.dot_general(
                split, keys, (((1,), (1,)), ((), ())), preferred_element_type=jnp.float32
            )
            expo = jnp.where(usable, jnp.exp((scores - 1.0) * scale), 0.0)
            total = jnp.sum(expo, axis=1, keepdims=True)
            mixed = dot(expo.astype(jnp.bfloat16), values) * (1.0 / total)
            result = jnp.zeros((window, cols), jnp.float32)
            for h, mine in enumerate(masks):
                result = jnp.where(mine, mixed[h * window : (h + 1) * window], result)
            framed[rows, at, :] = result.reshape(WL, WW, cols)
        for step in between.get(n, ()):
            advance(*step)

    for r in range(lat_rows):
        attended[r * lon : (r + 1) * lon, :] = turned(framed[WL - a + r], WW - b, lon)


def pieces(stack_rows, lat_first):
    sect, lat = lax.axis_index("sect"), lax.axis_index("lat")
    core, across, pair = lax.rem(sect, 2), sect // 2, lax.rem(lat, 2)
    step = stack_rows // 8
    by_lat, by_chip = {"lat": lat + 1 - 2 * pair}, {"sect": sect + 2 - 4 * across}
    by_core = {"sect": sect + 1 - 2 * core}
    if lat_first:
        outer, inner, targets = across, pair, [by_lat, by_chip, by_core]
    else:
        outer, inner, targets = pair, across, [by_chip, by_lat, by_core]
    ranges = [((core * 2 + outer) * 2 + inner, 1), (core * 2 + outer, 2), (core, 4)]
    at = [
        pl.ds(pl.multiple_of(index * (count * step), 16), count * step) for index, count in ranges
    ]
    return at, targets


def spread(stack, others, send_sem, recv_sem, lat_first):
    vars_, my_var, to_var, from_var = ring("var")
    at, targets = pieces(stack.shape[0], lat_first)
    groups = [
        [
            pltpu.make_async_remote_copy(
                src_ref=stack.at[at[0]],
                dst_ref=others.at[d - 1, at[0]],
                send_sem=send_sem.at[d - 1],
                recv_sem=recv_sem.at[d - 1],
                device_id={"var": to_var[d]},
                device_id_type=MESH,
            )
            for d in range(1, vars_)
        ]
    ]
    for k in range(3):
        groups.append(
            [
                pltpu.make_async_remote_copy(
                    src_ref=others.at[:, at[k]],
                    dst_ref=others.at[:, at[k]],
                    send_sem=send_sem.at[vars_ - 1 + k],
                    recv_sem=recv_sem.at[vars_ - 1 + k],
                    device_id=targets[k],
                    device_id_type=MESH,
                )
            ]
        )
    return groups


def advance(groups, stage):
    if stage:
        for copy in groups[stage - 1]:
            copy.wait()
    if stage < len(groups):
        for copy in groups[stage]:
            copy.start()


def feed(layer, attended, attended_in, stack, others, params, x_ref, out_ref, sems, phase, steps):
    vars_, my_var, to_var, from_var = ring("var")
    rows, heads_part = attended_in.shape[1:]
    width = x_ref.shape[2]

    def chosen(kind, position):
        index = (kind * 2 + layer) * 2 + position
        return jnp.concatenate([params[v, index : index + 1, :] for v in range(vars_)], axis=1)

    outgoing = []
    for d in range(1, vars_):
        at = pl.ds(pl.multiple_of(to_var[d] * rows, rows), rows)
        outgoing.append(
            send(attended.at[at], attended_in.at[d - 1], sems, phase, d, "var", to_var[d])
        )
    for step in steps[0]:
        advance(*step)
    own = attended[pl.ds(pl.multiple_of(my_var * rows, rows), rows), :]
    total = dot(own, stack[:heads_part])
    for d in range(1, vars_):
        outgoing[d - 1].wait()
        total = total + dot(attended_in[d - 1], others[d - 1, :heads_part])
    for step in steps[1]:
        advance(*step)
    mid = norm_add(x_ref[my_var], total, chosen(0, 0), chosen(1, 0))
    first = slice(heads_part, heads_part + width)
    shards = [stack] + [others.at[d] for d in range(vars_ - 1)]
    hidden = [
        jax.nn.gelu(dot(mid, shard[first]), approximate=True).astype(jnp.bfloat16)
        for shard in shards
    ]
    for step in steps[2]:
        advance(*step)
    total = jnp.zeros((rows, width), jnp.float32)
    for part, shard in zip(hidden, shards):
        total = total + dot(part, shard[heads_part + width :])
    out_ref[my_var] = norm_add(mid, total, chosen(0, 1), chosen(1, 1))


def whole_kernel(
    patches, table_hbm, wqkv_hbm, wout, w_in, w_out, scales, gains, biases, decode_hbm, shifts, out_ref,
    own_patch, table, wqkv, decode, load_sem,
    stack, patch_in, table_in, params_in, part, part_in, full, others, attended_in,
    q_ref, kv_ref, wide, q_shifted, kv_shifted, framed, attended,
    decode_in, made, landed, send_sem, recv_sem, halo_send, halo_recv, spread_send, spread_recv, patch_send, patch_recv,
):
    sems = (send_sem, recv_sem)
    sects, my_sect, to_sect, from_sect = ring("sect")
    vars_, my_var, to_var, from_var = ring("var")
    layers = wqkv.shape[0]
    lat_rows, lon_total, depth = patches.shape
    cols = lon_total // sects
    rows = full.shape[2]
    per = rows // cols
    for layer in range(layers):
        kv_ref[layer, :WL] = jnp.zeros_like(kv_ref[layer, :WL])
        kv_ref[layer, 2 * WL :] = jnp.zeros_like(kv_ref[layer, 2 * WL :])
    q_ref[...] = jnp.zeros_like(q_ref)
    own_cols = pl.ds(pl.multiple_of(my_sect * cols, cols), cols)
    pairs = []
    at = 0
    for weight in (wout, w_in, w_out):
        pairs.append((weight, stack.at[:, at : at + weight.shape[1], :]))
        at += weight.shape[1]
    pairs += [
        (table_hbm, table), (patches.at[:, own_cols, :], own_patch), (wqkv_hbm, wqkv),
        (decode_hbm, decode),
    ]
    loads = []
    for index, (source, target) in enumerate(pairs):
        loads.append(pltpu.make_async_copy(source, target, load_sem.at[index]))
        loads[-1].start()
    exists = lat_neighbours()
    barrier = pltpu.get_barrier_semaphore()
    my_lat = lax.axis_index("lat")
    for dl in (1, -1):
        @pl.when(exists[dl])
        def _():
            for ds in (0, 1, -1):
                target = {"sect": lax.rem(my_sect + ds + sects, sects), "lat": my_lat + dl}
                pl.semaphore_signal(barrier, inc=1, device_id=target, device_id_type=MESH)
    around = exists[1].astype(jnp.int32) + exists[-1].astype(jnp.int32)
    for axis, size, me in (("sect", sects, my_sect), ("var", vars_, my_var)):
        for d in range(1, size):
            pl.semaphore_signal(
                barrier, inc=1, device_id={axis: lax.rem(me + d, size)}, device_id_type=MESH
            )
    pl.semaphore_wait(barrier, sects + vars_ - 2 + 3 * around)

    last = 4 + 4 * layers
    later = []
    other_core = my_sect + 1 - 2 * lax.rem(my_sect, 2)
    other_chip = lax.rem(my_sect + 2, sects)

    def pass_table(source, owner, target, index):
        slot = lax.rem(target - owner + sects, sects) - 1
        return send(source, table_in.at[slot], sems, 0, index, "sect", target)

    tables = [pass_table(table_hbm, my_sect, other_chip, 0), pass_table(table_hbm, my_sect, other_core, 1)]
    chunks = []
    for k in range(vars_):
        lat = pl.ds(to_var[(k + 1) % vars_] * per, per)
        group = []
        for d in range(1, sects):
            at = pl.ds(pl.multiple_of(to_sect[d] * cols, cols), cols)
            copy = pltpu.make_async_remote_copy(
                src_ref=patches.at[lat, at, :],
                dst_ref=patch_in.at[d - 1, lat],
                send_sem=patch_send.at[k, d],
                recv_sem=patch_recv.at[k, d],
                device_id={"sect": to_sect[d]},
                device_id_type=MESH,
            )
            copy.start()
            group.append(copy)
        chunks.append(group)
    lines = gains.shape[0]
    params_in[my_var, :lines] = gains[...]
    params_in[my_var, lines:] = biases[...]
    for d in range(1, vars_):
        own = params_in.at[my_var]
        later.append(send(own, own, sems, 2, d, "var", to_var[d]))
    stack_rows = stack.shape[1]
    half = stack_rows - w_out.shape[1]
    carried = []
    for layer in range(layers):
        halves = [
            spread(
                stack.at[layer, at], others.at[layer, :, at],
                spread_send.at[layer, k], spread_recv.at[layer, k], k == 0,
            )
            for k, at in enumerate((slice(0, half), slice(half, stack_rows)))
        ]
        carried.append(halves)
    for load in loads[:3]:
        load.wait()
    advance(carried[0][0], 0)
    tables[0].wait()
    relayed = pass_table(table_in.at[sects // 2 - 1], other_chip, other_core, 2)
    for load in loads[3:]:
        load.wait()
    tables[1].wait()
    relayed.wait()
    weights = jnp.concatenate([table[...]] + [table_in[d] for d in range(sects - 1)], axis=0)

    def partial_of(owner):
        lat = pl.ds(owner * per, per)
        own = own_patch[lat]
        blocks = [own] + [patch_in[d, lat] for d in range(sects - 1)]
        x = jnp.concatenate([block.reshape(rows, depth) for block in blocks], axis=1)
        return dot(x, weights)

    outgoing = []
    for d in range(1, vars_):
        for copy in chunks[d - 1]:
            copy.wait()
        part[d - 1] = partial_of(to_var[d]).astype(jnp.bfloat16)
        outgoing.append(
            send(part.at[d - 1], part_in.at[d - 1], sems, 3, d, "var", to_var[d])
        )
    advance(carried[0][0], 1)
    for copy in chunks[vars_ - 1]:
        copy.wait()
    total = partial_of(my_var)
    for d in range(1, vars_):
        outgoing[d - 1].wait()
        total = total + part_in[d - 1].astype(jnp.float32)
    full[0, my_var] = total.astype(jnp.bfloat16)
    for d in range(1, sects):
        later.append(send(decode, decode_in.at[d - 1], sems, last, d, "sect", to_sect[d]))
    advance(carried[0][0], 2)
    for layer in range(layers):
        gather_project(
            full.at[layer], wqkv.at[layer], q_ref, kv_ref.at[layer], sems, 7 + 4 * layer,
            (halo_send.at[layer], halo_recv.at[layer]),
        )
        if layer == 0:
            for copy in later:
                copy.wait()
        early, late = carried[layer]
        ahead = carried[layer + 1] if layer + 1 < layers else None
        advance(early, 3)
        if layer == 0:
            advance(late, 0)
            between = {1: [(late, 1)], 3: [(late, 2)]}
        else:
            advance(late, 1)
            between = {1: [(late, 2)]}
        if ahead:
            advance(ahead[0], 0)
        attention(
            layer, shifts, scales, q_ref, kv_ref.at[layer], wide, q_shifted, kv_shifted,
            framed, attended.at[layer], between,
        )
        feed(
            layer, attended.at[layer], attended_in.at[layer], stack.at[layer], others.at[layer],
            params_in, full.at[layer], full.at[layer + 1], sems, 4 + 4 * layer,
            (
                [(early, 4)] + ([(ahead[0], 1)] if ahead else []),
                [(late, 3)] + ([(ahead[1], 0)] if ahead else []),
                [(late, 4)],
            ),
        )
        if ahead:
            advance(ahead[0], 2)
    stream = full.at[layers]
    outgoing = [
        send(stream.at[my_var], stream.at[my_var], sems, last + 1, d, "var", to_var[d])
        for d in range(1, vars_)
    ]
    weights = jnp.concatenate([decode[...]] + [decode_in[d] for d in range(sects - 1)], axis=1)
    copies = []
    for k in range(vars_):
        if k:
            outgoing[k - 1].wait()
        lat = pl.ds(from_var[k] * per, per)
        decoded = dot(stream[from_var[k]], weights).astype(jnp.bfloat16)
        for d in range(sects):
            block = decoded[:, d * depth : (d + 1) * depth].reshape(per, cols, depth)
            made[d, lat] = block
            if d:
                copies.append(
                    send(
                        made.at[d, lat], landed.at[sects - d, lat], sems, last + 2 + k, d, "sect",
                        from_sect[d],
                    )
                )
    out_ref[:, pl.ds(pl.multiple_of(my_sect * cols, cols), cols), :] = made[0]
    for copy in copies:
        copy.wait()
    for d in range(1, sects):
        at = pl.ds(pl.multiple_of(to_sect[d] * cols, cols), cols)
        out_ref[:, at, :] = landed[sects - d]


def per_device(
    patches,
    embed_weight,
    qkv_weight,
    out_weight,
    mlp_in_weight,
    mlp_out_weight,
    logit_scale,
    norm_gain,
    norm_bias,
    decode_weight,
    shifts,
):
    _, lat_rows, lon_total, patch_dim = patches.shape
    width = embed_weight.shape[2]
    layers, _, _, head_cols = qkv_weight.shape
    sects, vars_ = lax.axis_size("sect"), lax.axis_size("var")
    cols = lon_total // sects
    tokens = lat_rows * cols
    rows = tokens // vars_
    bf = jnp.bfloat16
    vmem = pl.BlockSpec(memory_space=pltpu.VMEM)
    smem = pl.BlockSpec(memory_space=pltpu.SMEM)
    hbm = pl.BlockSpec(memory_space=pltpu.HBM)
    wqkv = qkv_weight.transpose(0, 2, 1, 3)
    gains, biases = norm_gain.reshape(2 * layers, -1), norm_bias.reshape(2 * layers, -1)
    stack_rows = out_weight.shape[1] + mlp_in_weight.shape[1] + mlp_out_weight.shape[1]
    shards = pltpu.VMEM((vars_ - 1, rows, width), bf)
    ext_rows, ext_cols = lat_rows + 2 * WL, cols + 2 * WW
    phases = 4 + 4 * layers + 2 + vars_
    scratch = [
        pltpu.VMEM((lat_rows, cols, patch_dim), bf),
        pltpu.VMEM((patch_dim, width), bf),
        pltpu.VMEM((layers, 3, width, head_cols), bf),
        pltpu.VMEM((width, patch_dim), bf),
        pltpu.SemaphoreType.DMA((8,)),
        pltpu.VMEM((layers, stack_rows, width), bf),
        pltpu.VMEM((sects - 1, lat_rows, cols, patch_dim), bf),
        pltpu.VMEM((sects - 1, patch_dim, width), bf),
        pltpu.VMEM((vars_, 4 * layers, gains.shape[1]), jnp.float32),
        shards,
        shards,
        pltpu.VMEM((layers + 1, vars_, rows, width), bf),
        pltpu.VMEM((layers, vars_ - 1, stack_rows, width), bf),
        pltpu.VMEM((layers, vars_ - 1, rows, head_cols), bf),
        pltpu.VMEM((ext_rows, ext_cols, head_cols), jnp.float32),
        pltpu.VMEM((layers, ext_rows, ext_cols, 2 * head_cols), bf),
        pltpu.VMEM((ext_rows, ext_cols, 2 * head_cols), jnp.float32),
        pltpu.VMEM((lat_rows + WL, cols + WW, head_cols), bf),
        pltpu.VMEM((lat_rows + WL, cols + WW, 2 * head_cols), bf),
        pltpu.VMEM((lat_rows + WL, cols + WW, head_cols), jnp.float32),
        pltpu.VMEM((layers, tokens, head_cols), bf),
        pltpu.VMEM((sects - 1, width, patch_dim), bf),
        pltpu.VMEM((sects, lat_rows, cols, patch_dim), bf),
        pltpu.VMEM((sects, lat_rows, cols, patch_dim), bf),
        pltpu.SemaphoreType.DMA((phases, 4)),
        pltpu.SemaphoreType.DMA((phases, 4)),
        pltpu.SemaphoreType.DMA((layers, vars_, 8)),
        pltpu.SemaphoreType.DMA((layers, vars_, 8)),
        pltpu.SemaphoreType.DMA((layers, 2, vars_ + 2)),
        pltpu.SemaphoreType.DMA((layers, 2, vars_ + 2)),
        pltpu.SemaphoreType.DMA((vars_, sects)),
        pltpu.SemaphoreType.DMA((vars_, sects)),
    ]
    out = pl.pallas_call(
        whole_kernel,
        out_shape=jax.ShapeDtypeStruct((lat_rows, lon_total, patch_dim), bf),
        in_specs=[hbm] * 6 + [smem, vmem, vmem, hbm, smem],
        out_specs=vmem,
        scratch_shapes=scratch,
        compiler_params=pltpu.CompilerParams(
            collective_id=0, has_side_effects=True, vmem_limit_bytes=48 * 1024 * 1024
        ),
    )(
        patches[0], embed_weight[0], wqkv, out_weight, mlp_in_weight, mlp_out_weight,
        logit_scale, gains, biases, decode_weight[0], shifts,
    )
    return out[None]


def solution(mesh):
    return jax.shard_map(
        per_device,
        mesh=mesh,
        in_specs=(
            P(("sect", "var"), "lat", None, None),
            P(("sect", "var"), None, None),
            P(None, None, None, "var"),
            P(None, "var", None),
            P(None, None, "var"),
            P(None, "var", None),
            P(None, "var"),
            P(None, None, "var"),
            P(None, None, "var"),
            P(("sect", "var"), None, None),
            P(),
        ),
        out_specs=P(("sect", "var"), "lat", None, None),
        check_vma=False,
    )
```

```python
import jax
import jax.numpy as jnp
from jax import lax
from jax.experimental import pallas as pl
from jax.experimental.pallas import tpu as pltpu
from jax.sharding import PartitionSpec as P

WL = 8
WW = 16
HD = 64
MESH = pl.DeviceIdType.MESH

epsilon = 1e-06


def dot(a, b):
    return jnp.dot(a, b, preferred_element_type=jnp.float32)


def send(src, dst, sems, phase, d, axis, target):
    send_sem, recv_sem = sems
    copy = pltpu.make_async_remote_copy(
        src_ref=src,
        dst_ref=dst,
        send_sem=send_sem.at[phase, d],
        recv_sem=recv_sem.at[phase, d],
        device_id={axis: target},
        device_id_type=MESH,
    )
    copy.start()
    return copy


def ring(axis):
    size = lax.axis_size(axis)
    me = lax.axis_index(axis)
    after = [lax.rem(me + d, size) for d in range(size)]
    before = [lax.rem(me + size - d, size) for d in range(size)]
    return size, me, after, before


def head_unit(x):
    lane = lax.broadcasted_iota(jnp.int32, x.shape, 1)
    square = x * x
    inverse = jnp.zeros_like(x)
    for head in range(x.shape[1] // HD):
        mine = (lane >= head * HD) & (lane < (head + 1) * HD)
        total = jnp.sum(jnp.where(mine, square, 0.0), axis=1, keepdims=True)
        inverse = jnp.where(mine, lax.rsqrt(total + epsilon), inverse)
    return x * inverse


def project_chunk(x, wqkv, q_ref, kv_ref, owner):
    rows, cols = x.shape[0], q_ref.shape[2]
    lon = q_ref.shape[1] - 2 * WW
    per = rows // lon
    projected = dot(x, jnp.concatenate([wqkv[i] for i in range(3)], axis=1))
    lat = pl.ds(WL + owner * per, per)
    inner = slice(WW, WW + lon)
    q_ref[lat, inner, :] = head_unit(projected[:, :cols]).reshape(per, lon, cols)
    keys = head_unit(projected[:, cols : 2 * cols])
    paired = jnp.concatenate([keys, projected[:, 2 * cols :]], axis=1).astype(jnp.bfloat16)
    kv_ref[lat, inner, :] = paired.reshape(per, lon, 2 * cols)


def norm_add(stream, x, gain, bias):
    width = x.shape[1]
    mean = jnp.sum(x, axis=1, keepdims=True) / width
    variance = jnp.sum(x * x, axis=1, keepdims=True) / width - mean * mean
    normed = (x - mean) * lax.rsqrt(variance + 1e-05)
    return (stream.astype(jnp.float32) + gain * normed + bias).astype(jnp.bfloat16)


def gather_project(full, wqkv, q_ref, kv_ref, sems, phase, halo_sems):
    vars_, my_var, to_var, from_var = ring("var")
    outgoing = [
        send(full.at[my_var], full.at[my_var], sems, phase, d, "var", to_var[d])
        for d in range(1, vars_)
    ]
    per = full.shape[1] // (kv_ref.shape[1] - 2 * WW)
    copies = []
    for d in range(vars_):
        if d:
            outgoing[d - 1].wait()
        project_chunk(full[from_var[d]], wqkv, q_ref, kv_ref, from_var[d])
        copies += halo(kv_ref, from_var[d] * per, per, halo_sems, d)
    exists = lat_neighbours()
    for dl, copy in copies:
        if dl:
            pl.when(exists[dl])(copy.wait_send)
            pl.when(exists[-dl])(copy.wait_recv)
        else:
            copy.wait()


def lat_neighbours():
    size, me = lax.axis_size("lat"), lax.axis_index("lat")
    return {1: me < size - 1, -1: me > 0}


def halo(kv_ref, start, per, halo_sems, chunk):
    sects, my_sect = lax.axis_size("sect"), lax.axis_index("sect")
    my_lat = lax.axis_index("lat")
    lon = kv_ref.shape[1] - 2 * WW
    exists = lat_neighbours()
    taken = {0: slice(WW, WW + lon), 1: slice(lon, WW + lon), -1: slice(WW, 2 * WW)}
    placed = {0: slice(WW, WW + lon), 1: slice(0, WW), -1: slice(WW + lon, 2 * WW + lon)}
    landing = {0: WL, 1: 0, -1: 2 * WL}
    send_sem, recv_sem = halo_sems
    copies = []
    index = 0
    for dl in (1, -1, 0):
        for ds in (0, 1, -1):
            if dl == 0 and ds == 0:
                continue
            target = {"sect": lax.rem(my_sect + ds + sects, sects), "lat": my_lat + dl}
            copy = pltpu.make_async_remote_copy(
                src_ref=kv_ref.at[pl.ds(WL + start, per), taken[ds], :],
                dst_ref=kv_ref.at[pl.ds(landing[dl] + start, per), placed[ds], :],
                send_sem=send_sem.at[chunk, index],
                recv_sem=recv_sem.at[chunk, index],
                device_id=target,
                device_id_type=MESH,
            )
            index += 1
            copies.append((dl, copy))
            if dl:
                pl.when(exists[dl])(copy.start)
            else:
                copy.start()
    return copies


def attention(
    layer, shifts, scales, q_ref, kv_ref, wide, q_shifted, kv_shifted, framed, attended
):
    lat_rows, lon = WL, q_ref.shape[1] - 2 * WW
    cols = q_ref.shape[2]
    a, b = shifts[layer, 0], shifts[layer, 1]
    my_lat, lats = lax.axis_index("lat"), lax.axis_size("lat")
    wide[...] = kv_ref[...].astype(jnp.float32)
    frame_rows, frame_cols = lat_rows + WL, lon + WW

    def turned(row, step, length):
        return pltpu.roll(row, row.shape[0] - step, 0)[:length].astype(jnp.bfloat16)

    for r in range(frame_rows):
        kv_shifted[r] = turned(wide[a + r], b, frame_cols)
        q_shifted[r] = turned(q_ref[a + r], b, frame_cols)
    heads, window = cols // HD, WL * WW
    lane = lax.broadcasted_iota(jnp.int32, (window, cols), 1)
    key_row = lax.broadcasted_iota(jnp.int32, (heads * window, window), 1) // WW
    head_row = lax.broadcasted_iota(jnp.int32, (heads * window, window), 0) // window
    scale = jnp.zeros((heads * window, window), jnp.float32)
    for h in range(heads):
        scale = jnp.where(head_row == h, scales[layer, h], scale)
    masks = [(lane >= h * HD) & (lane < (h + 1) * HD) for h in range(heads)]

    for n in range(frame_cols // WW):
        at = slice(n * WW, (n + 1) * WW)
        for m in range(frame_rows // WL):
            rows = slice(m * WL, (m + 1) * WL)
            queries = q_shifted[rows, at, :].reshape(window, cols)
            paired = kv_shifted[rows, at, :].reshape(window, 2 * cols)
            keys, values = paired[:, :cols], paired[:, cols:]
            place = my_lat * lat_rows - WL + a + m * WL + key_row
            usable = (place >= 0) & (place < lats * lat_rows)
            split = jnp.concatenate(
                [jnp.where(mine, queries, jnp.zeros_like(queries)) for mine in masks], axis=0
            )
            scores = lax.dot_general(
                split, keys, (((1,), (1,)), ((), ())), preferred_element_type=jnp.float32
            )
            expo = jnp.where(usable, jnp.exp((scores - 1.0) * scale), 0.0)
            total = jnp.sum(expo, axis=1, keepdims=True)
            mixed = dot(expo.astype(jnp.bfloat16), values) * (1.0 / total)
            result = jnp.zeros((window, cols), jnp.float32)
            for h, mine in enumerate(masks):
                result = jnp.where(mine, mixed[h * window : (h + 1) * window], result)
            framed[rows, at, :] = result.reshape(WL, WW, cols)

    for r in range(lat_rows):
        attended[r * lon : (r + 1) * lon, :] = turned(framed[WL - a + r], WW - b, lon)


def pieces(stack_rows, lat_first):
    sect, lat = lax.axis_index("sect"), lax.axis_index("lat")
    core, across, pair = lax.rem(sect, 2), sect // 2, lax.rem(lat, 2)
    step = stack_rows // 8
    by_lat, by_chip = {"lat": lat + 1 - 2 * pair}, {"sect": sect + 2 - 4 * across}
    by_core = {"sect": sect + 1 - 2 * core}
    if lat_first:
        outer, inner, targets = across, pair, [by_lat, by_chip, by_core]
    else:
        outer, inner, targets = pair, across, [by_chip, by_lat, by_core]
    ranges = [((core * 2 + outer) * 2 + inner, 1), (core * 2 + outer, 2), (core, 4)]
    at = [
        pl.ds(pl.multiple_of(index * (count * step), 16), count * step) for index, count in ranges
    ]
    return at, targets


def spread(stack, others, send_sem, recv_sem, lat_first):
    vars_, my_var, to_var, from_var = ring("var")
    at, targets = pieces(stack.shape[0], lat_first)
    groups = [
        [
            pltpu.make_async_remote_copy(
                src_ref=stack.at[at[0]],
                dst_ref=others.at[d - 1, at[0]],
                send_sem=send_sem.at[d - 1],
                recv_sem=recv_sem.at[d - 1],
                device_id={"var": to_var[d]},
                device_id_type=MESH,
            )
            for d in range(1, vars_)
        ]
    ]
    for k in range(3):
        groups.append(
            [
                pltpu.make_async_remote_copy(
                    src_ref=others.at[:, at[k]],
                    dst_ref=others.at[:, at[k]],
                    send_sem=send_sem.at[vars_ - 1 + k],
                    recv_sem=recv_sem.at[vars_ - 1 + k],
                    device_id=targets[k],
                    device_id_type=MESH,
                )
            ]
        )
    return groups


def advance(groups, stage):
    if stage:
        for copy in groups[stage - 1]:
            copy.wait()
    if stage < len(groups):
        for copy in groups[stage]:
            copy.start()


def feed(layer, attended, attended_in, stack, others, params, x_ref, out_ref, sems, phase, steps):
    vars_, my_var, to_var, from_var = ring("var")
    rows, heads_part = attended_in.shape[1:]
    width = x_ref.shape[2]

    def chosen(kind, position):
        index = (kind * 2 + layer) * 2 + position
        return jnp.concatenate([params[v, index : index + 1, :] for v in range(vars_)], axis=1)

    outgoing = []
    for d in range(1, vars_):
        at = pl.ds(pl.multiple_of(to_var[d] * rows, rows), rows)
        outgoing.append(
            send(attended.at[at], attended_in.at[d - 1], sems, phase, d, "var", to_var[d])
        )
    for step in steps[0]:
        advance(*step)
    own = attended[pl.ds(pl.multiple_of(my_var * rows, rows), rows), :]
    total = dot(own, stack[:heads_part])
    for d in range(1, vars_):
        outgoing[d - 1].wait()
        total = total + dot(attended_in[d - 1], others[d - 1, :heads_part])
    for step in steps[1]:
        advance(*step)
    mid = norm_add(x_ref[my_var], total, chosen(0, 0), chosen(1, 0))
    first = slice(heads_part, heads_part + width)
    shards = [stack] + [others.at[d] for d in range(vars_ - 1)]
    hidden = [
        jax.nn.gelu(dot(mid, shard[first]), approximate=True).astype(jnp.bfloat16)
        for shard in shards
    ]
    for step in steps[2]:
        advance(*step)
    total = jnp.zeros((rows, width), jnp.float32)
    for part, shard in zip(hidden, shards):
        total = total + dot(part, shard[heads_part + width :])
    out_ref[my_var] = norm_add(mid, total, chosen(0, 1), chosen(1, 1))


def whole_kernel(
    patches, table_hbm, wqkv_hbm, wout, w_in, w_out, scales, gains, biases, decode_hbm, shifts, out_ref,
    own_patch, table, wqkv, decode, load_sem,
    stack, patch_in, table_in, params_in, part, part_in, full, others, attended_in,
    q_ref, kv_ref, wide, q_shifted, kv_shifted, framed, attended,
    decode_in, made, landed, send_sem, recv_sem, halo_send, halo_recv, spread_send, spread_recv, patch_send, patch_recv,
):
    sems = (send_sem, recv_sem)
    sects, my_sect, to_sect, from_sect = ring("sect")
    vars_, my_var, to_var, from_var = ring("var")
    layers = wqkv.shape[0]
    lat_rows, lon_total, depth = patches.shape
    cols = lon_total // sects
    rows = full.shape[2]
    per = rows // cols
    for layer in range(layers):
        kv_ref[layer, :WL] = jnp.zeros_like(kv_ref[layer, :WL])
        kv_ref[layer, 2 * WL :] = jnp.zeros_like(kv_ref[layer, 2 * WL :])
    q_ref[...] = jnp.zeros_like(q_ref)
    own_cols = pl.ds(pl.multiple_of(my_sect * cols, cols), cols)
    pairs = []
    at = 0
    for weight in (wout, w_in, w_out):
        pairs.append((weight, stack.at[:, at : at + weight.shape[1], :]))
        at += weight.shape[1]
    pairs += [
        (table_hbm, table), (patches.at[:, own_cols, :], own_patch), (wqkv_hbm, wqkv),
        (decode_hbm, decode),
    ]
    loads = []
    for index, (source, target) in enumerate(pairs):
        loads.append(pltpu.make_async_copy(source, target, load_sem.at[index]))
        loads[-1].start()
    exists = lat_neighbours()
    barrier = pltpu.get_barrier_semaphore()
    my_lat = lax.axis_index("lat")
    for dl in (1, -1):
        @pl.when(exists[dl])
        def _():
            for ds in (0, 1, -1):
                target = {"sect": lax.rem(my_sect + ds + sects, sects), "lat": my_lat + dl}
                pl.semaphore_signal(barrier, inc=1, device_id=target, device_id_type=MESH)
    around = exists[1].astype(jnp.int32) + exists[-1].astype(jnp.int32)
    for axis, size, me in (("sect", sects, my_sect), ("var", vars_, my_var)):
        for d in range(1, size):
            pl.semaphore_signal(
                barrier, inc=1, device_id={axis: lax.rem(me + d, size)}, device_id_type=MESH
            )
    pl.semaphore_wait(barrier, sects + vars_ - 2 + 3 * around)

    last = 4 + 4 * layers
    later = []
    other_core = my_sect + 1 - 2 * lax.rem(my_sect, 2)
    other_chip = lax.rem(my_sect + 2, sects)

    def pass_table(source, owner, target, index):
        slot = lax.rem(target - owner + sects, sects) - 1
        return send(source, table_in.at[slot], sems, 0, index, "sect", target)

    tables = [pass_table(table_hbm, my_sect, other_chip, 0), pass_table(table_hbm, my_sect, other_core, 1)]
    chunks = []
    for k in range(vars_):
        lat = pl.ds(to_var[(k + 1) % vars_] * per, per)
        group = []
        for d in range(1, sects):
            at = pl.ds(pl.multiple_of(to_sect[d] * cols, cols), cols)
            copy = pltpu.make_async_remote_copy(
                src_ref=patches.at[lat, at, :],
                dst_ref=patch_in.at[d - 1, lat],
                send_sem=patch_send.at[k, d],
                recv_sem=patch_recv.at[k, d],
                device_id={"sect": to_sect[d]},
                device_id_type=MESH,
            )
            copy.start()
            group.append(copy)
        chunks.append(group)
    lines = gains.shape[0]
    params_in[my_var, :lines] = gains[...]
    params_in[my_var, lines:] = biases[...]
    for d in range(1, vars_):
        own = params_in.at[my_var]
        later.append(send(own, own, sems, 2, d, "var", to_var[d]))
    stack_rows = stack.shape[1]
    half = stack_rows - w_out.shape[1]
    carried = []
    for layer in range(layers):
        halves = [
            spread(
                stack.at[layer, at], others.at[layer, :, at],
                spread_send.at[layer, k], spread_recv.at[layer, k], k == 0,
            )
            for k, at in enumerate((slice(0, half), slice(half, stack_rows)))
        ]
        carried.append(halves)
    for load in loads[:3]:
        load.wait()
    for half_gather in carried[0]:
        advance(half_gather, 0)
    tables[0].wait()
    relayed = pass_table(table_in.at[sects // 2 - 1], other_chip, other_core, 2)
    for load in loads[3:]:
        load.wait()
    tables[1].wait()
    relayed.wait()
    weights = jnp.concatenate([table[...]] + [table_in[d] for d in range(sects - 1)], axis=0)

    def partial_of(owner):
        lat = pl.ds(owner * per, per)
        own = own_patch[lat]
        blocks = [own] + [patch_in[d, lat] for d in range(sects - 1)]
        x = jnp.concatenate([block.reshape(rows, depth) for block in blocks], axis=1)
        return dot(x, weights)

    outgoing = []
    for d in range(1, vars_):
        for copy in chunks[d - 1]:
            copy.wait()
        part[d - 1] = partial_of(to_var[d]).astype(jnp.bfloat16)
        outgoing.append(
            send(part.at[d - 1], part_in.at[d - 1], sems, 3, d, "var", to_var[d])
        )
    for half_gather in carried[0]:
        advance(half_gather, 1)
    for copy in chunks[vars_ - 1]:
        copy.wait()
    total = partial_of(my_var)
    for d in range(1, vars_):
        outgoing[d - 1].wait()
        total = total + part_in[d - 1].astype(jnp.float32)
    full[0, my_var] = total.astype(jnp.bfloat16)
    for d in range(1, sects):
        later.append(send(decode, decode_in.at[d - 1], sems, last, d, "sect", to_sect[d]))
    for half_gather in carried[0]:
        advance(half_gather, 2)
    for layer in range(layers):
        gather_project(
            full.at[layer], wqkv.at[layer], q_ref, kv_ref.at[layer], sems, 7 + 4 * layer,
            (halo_send.at[layer], halo_recv.at[layer]),
        )
        if layer == 0:
            for copy in later:
                copy.wait()
        early, late = carried[layer]
        ahead = carried[layer + 1] if layer + 1 < layers else []
        advance(early, 3)
        advance(late, 3)
        for half_gather in ahead:
            advance(half_gather, 0)
        attention(
            layer, shifts, scales, q_ref, kv_ref.at[layer], wide, q_shifted, kv_shifted,
            framed, attended.at[layer],
        )
        feed(
            layer, attended.at[layer], attended_in.at[layer], stack.at[layer], others.at[layer],
            params_in, full.at[layer], full.at[layer + 1], sems, 4 + 4 * layer,
            ([(early, 4)], [(half_gather, 1) for half_gather in ahead], [(late, 4)]),
        )
        for half_gather in ahead:
            advance(half_gather, 2)
    stream = full.at[layers]
    outgoing = [
        send(stream.at[my_var], stream.at[my_var], sems, last + 1, d, "var", to_var[d])
        for d in range(1, vars_)
    ]
    weights = jnp.concatenate([decode[...]] + [decode_in[d] for d in range(sects - 1)], axis=1)
    copies = []
    for k in range(vars_):
        if k:
            outgoing[k - 1].wait()
        lat = pl.ds(from_var[k] * per, per)
        decoded = dot(stream[from_var[k]], weights).astype(jnp.bfloat16)
        for d in range(sects):
            block = decoded[:, d * depth : (d + 1) * depth].reshape(per, cols, depth)
            made[d, lat] = block
            if d:
                copies.append(
                    send(
                        made.at[d, lat], landed.at[sects - d, lat], sems, last + 2 + k, d, "sect",
                        from_sect[d],
                    )
                )
    out_ref[:, pl.ds(pl.multiple_of(my_sect * cols, cols), cols), :] = made[0]
    for copy in copies:
        copy.wait()
    for d in range(1, sects):
        at = pl.ds(pl.multiple_of(to_sect[d] * cols, cols), cols)
        out_ref[:, at, :] = landed[sects - d]


def per_device(
    patches,
    embed_weight,
    qkv_weight,
    out_weight,
    mlp_in_weight,
    mlp_out_weight,
    logit_scale,
    norm_gain,
    norm_bias,
    decode_weight,
    shifts,
):
    _, lat_rows, lon_total, patch_dim = patches.shape
    width = embed_weight.shape[2]
    layers, _, _, head_cols = qkv_weight.shape
    sects, vars_ = lax.axis_size("sect"), lax.axis_size("var")
    cols = lon_total // sects
    tokens = lat_rows * cols
    rows = tokens // vars_
    bf = jnp.bfloat16
    vmem = pl.BlockSpec(memory_space=pltpu.VMEM)
    smem = pl.BlockSpec(memory_space=pltpu.SMEM)
    hbm = pl.BlockSpec(memory_space=pltpu.HBM)
    wqkv = qkv_weight.transpose(0, 2, 1, 3)
    gains, biases = norm_gain.reshape(2 * layers, -1), norm_bias.reshape(2 * layers, -1)
    stack_rows = out_weight.shape[1] + mlp_in_weight.shape[1] + mlp_out_weight.shape[1]
    shards = pltpu.VMEM((vars_ - 1, rows, width), bf)
    ext_rows, ext_cols = lat_rows + 2 * WL, cols + 2 * WW
    phases = 4 + 4 * layers + 2 + vars_
    scratch = [
        pltpu.VMEM((lat_rows, cols, patch_dim), bf),
        pltpu.VMEM((patch_dim, width), bf),
        pltpu.VMEM((layers, 3, width, head_cols), bf),
        pltpu.VMEM((width, patch_dim), bf),
        pltpu.SemaphoreType.DMA((8,)),
        pltpu.VMEM((layers, stack_rows, width), bf),
        pltpu.VMEM((sects - 1, lat_rows, cols, patch_dim), bf),
        pltpu.VMEM((sects - 1, patch_dim, width), bf),
        pltpu.VMEM((vars_, 4 * layers, gains.shape[1]), jnp.float32),
        shards,
        shards,
        pltpu.VMEM((layers + 1, vars_, rows, width), bf),
        pltpu.VMEM((layers, vars_ - 1, stack_rows, width), bf),
        pltpu.VMEM((layers, vars_ - 1, rows, head_cols), bf),
        pltpu.VMEM((ext_rows, ext_cols, head_cols), jnp.float32),
        pltpu.VMEM((layers, ext_rows, ext_cols, 2 * head_cols), bf),
        pltpu.VMEM((ext_rows, ext_cols, 2 * head_cols), jnp.float32),
        pltpu.VMEM((lat_rows + WL, cols + WW, head_cols), bf),
        pltpu.VMEM((lat_rows + WL, cols + WW, 2 * head_cols), bf),
        pltpu.VMEM((lat_rows + WL, cols + WW, head_cols), jnp.float32),
        pltpu.VMEM((layers, tokens, head_cols), bf),
        pltpu.VMEM((sects - 1, width, patch_dim), bf),
        pltpu.VMEM((sects, lat_rows, cols, patch_dim), bf),
        pltpu.VMEM((sects, lat_rows, cols, patch_dim), bf),
        pltpu.SemaphoreType.DMA((phases, 4)),
        pltpu.SemaphoreType.DMA((phases, 4)),
        pltpu.SemaphoreType.DMA((layers, vars_, 8)),
        pltpu.SemaphoreType.DMA((layers, vars_, 8)),
        pltpu.SemaphoreType.DMA((layers, 2, vars_ + 2)),
        pltpu.SemaphoreType.DMA((layers, 2, vars_ + 2)),
        pltpu.SemaphoreType.DMA((vars_, sects)),
        pltpu.SemaphoreType.DMA((vars_, sects)),
    ]
    out = pl.pallas_call(
        whole_kernel,
        out_shape=jax.ShapeDtypeStruct((lat_rows, lon_total, patch_dim), bf),
        in_specs=[hbm] * 6 + [smem, vmem, vmem, hbm, smem],
        out_specs=vmem,
        scratch_shapes=scratch,
        compiler_params=pltpu.CompilerParams(
            collective_id=0, has_side_effects=True, vmem_limit_bytes=64 * 1024 * 1024 - 65536
        ),
    )(
        patches[0], embed_weight[0], wqkv, out_weight, mlp_in_weight, mlp_out_weight,
        logit_scale, gains, biases, decode_weight[0], shifts,
    )
    return out[None]


def solution(mesh):
    return jax.shard_map(
        per_device,
        mesh=mesh,
        in_specs=(
            P(("sect", "var"), "lat", None, None),
            P(("sect", "var"), None, None),
            P(None, None, None, "var"),
            P(None, "var", None),
            P(None, None, "var"),
            P(None, "var", None),
            P(None, "var"),
            P(None, None, "var"),
            P(None, None, "var"),
            P(("sect", "var"), None, None),
            P(),
        ),
        out_specs=P(("sect", "var"), "lat", None, None),
        check_vma=False,
    )
```

```python
import jax
import jax.numpy as jnp
from jax import lax
from jax.experimental import pallas as pl
from jax.experimental.pallas import tpu as pltpu
from jax.sharding import PartitionSpec as P

WL = 8
WW = 16
HD = 64
MESH = pl.DeviceIdType.MESH

epsilon = 1e-06


def dot(a, b):
    return jnp.dot(a, b, preferred_element_type=jnp.float32)


def send(src, dst, sems, phase, d, axis, target):
    send_sem, recv_sem = sems
    copy = pltpu.make_async_remote_copy(
        src_ref=src,
        dst_ref=dst,
        send_sem=send_sem.at[phase, d],
        recv_sem=recv_sem.at[phase, d],
        device_id={axis: target},
        device_id_type=MESH,
    )
    copy.start()
    return copy


def ring(axis):
    size = lax.axis_size(axis)
    me = lax.axis_index(axis)
    after = [lax.rem(me + d, size) for d in range(size)]
    before = [lax.rem(me + size - d, size) for d in range(size)]
    return size, me, after, before


def head_unit(x):
    lane = lax.broadcasted_iota(jnp.int32, x.shape, 1)
    square = x * x
    inverse = jnp.zeros_like(x)
    for head in range(x.shape[1] // HD):
        mine = (lane >= head * HD) & (lane < (head + 1) * HD)
        total = jnp.sum(jnp.where(mine, square, 0.0), axis=1, keepdims=True)
        inverse = jnp.where(mine, lax.rsqrt(total + epsilon), inverse)
    return x * inverse


def project_chunk(x, wqkv, q_ref, kv_ref, owner):
    rows, cols = x.shape[0], q_ref.shape[2]
    lon = q_ref.shape[1] - 2 * WW
    per = rows // lon
    projected = dot(x, jnp.concatenate([wqkv[i] for i in range(3)], axis=1))
    lat = pl.ds(WL + owner * per, per)
    inner = slice(WW, WW + lon)
    q_ref[lat, inner, :] = head_unit(projected[:, :cols]).reshape(per, lon, cols)
    keys = head_unit(projected[:, cols : 2 * cols])
    paired = jnp.concatenate([keys, projected[:, 2 * cols :]], axis=1).astype(jnp.bfloat16)
    kv_ref[lat, inner, :] = paired.reshape(per, lon, 2 * cols)


def norm_add(stream, x, gain, bias):
    width = x.shape[1]
    mean = jnp.sum(x, axis=1, keepdims=True) / width
    variance = jnp.sum(x * x, axis=1, keepdims=True) / width - mean * mean
    normed = (x - mean) * lax.rsqrt(variance + 1e-05)
    return (stream.astype(jnp.float32) + gain * normed + bias).astype(jnp.bfloat16)


def gather_project(full, wqkv, q_ref, kv_ref, sems, phase, halo_sems):
    vars_, my_var, to_var, from_var = ring("var")
    outgoing = [
        send(full.at[my_var], full.at[my_var], sems, phase, d, "var", to_var[d])
        for d in range(1, vars_)
    ]
    per = full.shape[1] // (kv_ref.shape[1] - 2 * WW)
    copies = []
    for d in range(vars_):
        if d:
            outgoing[d - 1].wait()
        project_chunk(full[from_var[d]], wqkv, q_ref, kv_ref, from_var[d])
        copies += halo(kv_ref, from_var[d] * per, per, halo_sems, d)
    exists = lat_neighbours()
    for dl, copy in copies:
        if dl:
            pl.when(exists[dl])(copy.wait_send)
            pl.when(exists[-dl])(copy.wait_recv)
        else:
            copy.wait()


def lat_neighbours():
    size, me = lax.axis_size("lat"), lax.axis_index("lat")
    return {1: me < size - 1, -1: me > 0}


def halo(kv_ref, start, per, halo_sems, chunk):
    sects, my_sect = lax.axis_size("sect"), lax.axis_index("sect")
    my_lat = lax.axis_index("lat")
    lon = kv_ref.shape[1] - 2 * WW
    exists = lat_neighbours()
    taken = {0: slice(WW, WW + lon), 1: slice(lon, WW + lon), -1: slice(WW, 2 * WW)}
    placed = {0: slice(WW, WW + lon), 1: slice(0, WW), -1: slice(WW + lon, 2 * WW + lon)}
    landing = {0: WL, 1: 0, -1: 2 * WL}
    send_sem, recv_sem = halo_sems
    copies = []
    index = 0
    for dl in (1, -1, 0):
        for ds in (0, 1, -1):
            if dl == 0 and ds == 0:
                continue
            target = {"sect": lax.rem(my_sect + ds + sects, sects), "lat": my_lat + dl}
            copy = pltpu.make_async_remote_copy(
                src_ref=kv_ref.at[pl.ds(WL + start, per), taken[ds], :],
                dst_ref=kv_ref.at[pl.ds(landing[dl] + start, per), placed[ds], :],
                send_sem=send_sem.at[chunk, index],
                recv_sem=recv_sem.at[chunk, index],
                device_id=target,
                device_id_type=MESH,
            )
            index += 1
            copies.append((dl, copy))
            if dl:
                pl.when(exists[dl])(copy.start)
            else:
                copy.start()
    return copies


def attention(
    layer, shifts, scales, q_ref, kv_ref, wide, q_shifted, kv_shifted, framed, attended
):
    lat_rows, lon = WL, q_ref.shape[1] - 2 * WW
    cols = q_ref.shape[2]
    a, b = shifts[layer, 0], shifts[layer, 1]
    my_lat, lats = lax.axis_index("lat"), lax.axis_size("lat")
    wide[...] = kv_ref[...].astype(jnp.float32)
    frame_rows, frame_cols = lat_rows + WL, lon + WW

    def turned(row, step, length):
        return pltpu.roll(row, row.shape[0] - step, 0)[:length].astype(jnp.bfloat16)

    for r in range(frame_rows):
        kv_shifted[r] = turned(wide[a + r], b, frame_cols)
        q_shifted[r] = turned(q_ref[a + r], b, frame_cols)
    heads, window = cols // HD, WL * WW
    lane = lax.broadcasted_iota(jnp.int32, (window, cols), 1)
    key_row = lax.broadcasted_iota(jnp.int32, (heads * window, window), 1) // WW
    head_row = lax.broadcasted_iota(jnp.int32, (heads * window, window), 0) // window
    scale = jnp.zeros((heads * window, window), jnp.float32)
    for h in range(heads):
        scale = jnp.where(head_row == h, scales[layer, h], scale)
    masks = [(lane >= h * HD) & (lane < (h + 1) * HD) for h in range(heads)]

    for n in range(frame_cols // WW):
        at = slice(n * WW, (n + 1) * WW)
        for m in range(frame_rows // WL):
            rows = slice(m * WL, (m + 1) * WL)
            queries = q_shifted[rows, at, :].reshape(window, cols)
            paired = kv_shifted[rows, at, :].reshape(window, 2 * cols)
            keys, values = paired[:, :cols], paired[:, cols:]
            place = my_lat * lat_rows - WL + a + m * WL + key_row
            usable = (place >= 0) & (place < lats * lat_rows)
            split = jnp.concatenate(
                [jnp.where(mine, queries, jnp.zeros_like(queries)) for mine in masks], axis=0
            )
            scores = lax.dot_general(
                split, keys, (((1,), (1,)), ((), ())), preferred_element_type=jnp.float32
            )
            expo = jnp.where(usable, jnp.exp((scores - 1.0) * scale), 0.0)
            total = jnp.sum(expo, axis=1, keepdims=True)
            mixed = dot(expo.astype(jnp.bfloat16), values) * (1.0 / total)
            result = jnp.zeros((window, cols), jnp.float32)
            for h, mine in enumerate(masks):
                result = jnp.where(mine, mixed[h * window : (h + 1) * window], result)
            framed[rows, at, :] = result.reshape(WL, WW, cols)

    for r in range(lat_rows):
        attended[r * lon : (r + 1) * lon, :] = turned(framed[WL - a + r], WW - b, lon)


def pieces(stack_rows, lat_first):
    sect, lat = lax.axis_index("sect"), lax.axis_index("lat")
    core, across, pair = lax.rem(sect, 2), sect // 2, lax.rem(lat, 2)
    step = stack_rows // 8
    by_lat, by_chip = {"lat": lat + 1 - 2 * pair}, {"sect": sect + 2 - 4 * across}
    by_core = {"sect": sect + 1 - 2 * core}
    if lat_first:
        outer, inner, targets = across, pair, [by_lat, by_chip, by_core]
    else:
        outer, inner, targets = pair, across, [by_chip, by_lat, by_core]
    ranges = [((core * 2 + outer) * 2 + inner, 1), (core * 2 + outer, 2), (core, 4)]
    at = [
        pl.ds(pl.multiple_of(index * (count * step), 16), count * step) for index, count in ranges
    ]
    return at, targets


def spread(stack, others, send_sem, recv_sem, lat_first):
    vars_, my_var, to_var, from_var = ring("var")
    at, targets = pieces(stack.shape[0], lat_first)
    groups = [
        [
            pltpu.make_async_remote_copy(
                src_ref=stack.at[at[0]],
                dst_ref=others.at[d - 1, at[0]],
                send_sem=send_sem.at[d - 1],
                recv_sem=recv_sem.at[d - 1],
                device_id={"var": to_var[d]},
                device_id_type=MESH,
            )
            for d in range(1, vars_)
        ]
    ]
    for k in range(3):
        groups.append(
            [
                pltpu.make_async_remote_copy(
                    src_ref=others.at[:, at[k]],
                    dst_ref=others.at[:, at[k]],
                    send_sem=send_sem.at[vars_ - 1 + k],
                    recv_sem=recv_sem.at[vars_ - 1 + k],
                    device_id=targets[k],
                    device_id_type=MESH,
                )
            ]
        )
    return groups


def advance(groups, stage):
    if stage:
        for copy in groups[stage - 1]:
            copy.wait()
    if stage < len(groups):
        for copy in groups[stage]:
            copy.start()


def feed(layer, attended, attended_in, stack, others, params, x_ref, out_ref, sems, phase, steps):
    vars_, my_var, to_var, from_var = ring("var")
    rows, heads_part = attended_in.shape[1:]
    width = x_ref.shape[2]

    def chosen(kind, position):
        index = (kind * 2 + layer) * 2 + position
        return jnp.concatenate([params[v, index : index + 1, :] for v in range(vars_)], axis=1)

    outgoing = []
    for d in range(1, vars_):
        at = pl.ds(pl.multiple_of(to_var[d] * rows, rows), rows)
        outgoing.append(
            send(attended.at[at], attended_in.at[d - 1], sems, phase, d, "var", to_var[d])
        )
    for step in steps[0]:
        advance(*step)
    own = attended[pl.ds(pl.multiple_of(my_var * rows, rows), rows), :]
    total = dot(own, stack[:heads_part])
    for d in range(1, vars_):
        outgoing[d - 1].wait()
        total = total + dot(attended_in[d - 1], others[d - 1, :heads_part])
    for step in steps[1]:
        advance(*step)
    mid = norm_add(x_ref[my_var], total, chosen(0, 0), chosen(1, 0))
    first = slice(heads_part, heads_part + width)
    shards = [stack] + [others.at[d] for d in range(vars_ - 1)]
    hidden = [
        jax.nn.gelu(dot(mid, shard[first]), approximate=True).astype(jnp.bfloat16)
        for shard in shards
    ]
    for step in steps[2]:
        advance(*step)
    total = jnp.zeros((rows, width), jnp.float32)
    for part, shard in zip(hidden, shards):
        total = total + dot(part, shard[heads_part + width :])
    out_ref[my_var] = norm_add(mid, total, chosen(0, 1), chosen(1, 1))


def whole_kernel(
    patches, table_hbm, wqkv_hbm, wout, w_in, w_out, scales, gains, biases, decode_hbm, shifts, out_ref,
    own_patch, table, wqkv, decode, load_sem,
    stack, patch_in, table_in, params_in, part, part_in, full, others, attended_in,
    q_ref, kv_ref, wide, q_shifted, kv_shifted, framed, attended,
    decode_in, made, landed, send_sem, recv_sem, halo_send, halo_recv, spread_send, spread_recv, patch_send, patch_recv,
):
    sems = (send_sem, recv_sem)
    sects, my_sect, to_sect, from_sect = ring("sect")
    vars_, my_var, to_var, from_var = ring("var")
    layers = wqkv.shape[0]
    lat_rows, lon_total, depth = patches.shape
    cols = lon_total // sects
    rows = full.shape[2]
    per = rows // cols
    for layer in range(layers):
        kv_ref[layer, :WL] = jnp.zeros_like(kv_ref[layer, :WL])
        kv_ref[layer, 2 * WL :] = jnp.zeros_like(kv_ref[layer, 2 * WL :])
    q_ref[...] = jnp.zeros_like(q_ref)
    own_cols = pl.ds(pl.multiple_of(my_sect * cols, cols), cols)
    pairs = []
    at = 0
    for weight in (wout, w_in, w_out):
        pairs.append((weight, stack.at[:, at : at + weight.shape[1], :]))
        at += weight.shape[1]
    pairs += [
        (table_hbm, table), (patches.at[:, own_cols, :], own_patch), (wqkv_hbm, wqkv),
        (decode_hbm, decode),
    ]
    loads = []
    for index, (source, target) in enumerate(pairs):
        loads.append(pltpu.make_async_copy(source, target, load_sem.at[index]))
        loads[-1].start()
    exists = lat_neighbours()
    barrier = pltpu.get_barrier_semaphore()
    my_lat = lax.axis_index("lat")
    for dl in (1, -1):
        @pl.when(exists[dl])
        def _():
            for ds in (0, 1, -1):
                target = {"sect": lax.rem(my_sect + ds + sects, sects), "lat": my_lat + dl}
                pl.semaphore_signal(barrier, inc=1, device_id=target, device_id_type=MESH)
    around = exists[1].astype(jnp.int32) + exists[-1].astype(jnp.int32)
    for axis, size, me in (("sect", sects, my_sect), ("var", vars_, my_var)):
        for d in range(1, size):
            pl.semaphore_signal(
                barrier, inc=1, device_id={axis: lax.rem(me + d, size)}, device_id_type=MESH
            )
    pl.semaphore_wait(barrier, sects + vars_ - 2 + 3 * around)

    last = 4 + 4 * layers
    later = []
    other_core = my_sect + 1 - 2 * lax.rem(my_sect, 2)
    other_chip = lax.rem(my_sect + 2, sects)

    def pass_table(source, owner, target, index):
        slot = lax.rem(target - owner + sects, sects) - 1
        return send(source, table_in.at[slot], sems, 0, index, "sect", target)

    tables = [pass_table(table_hbm, my_sect, other_chip, 0), pass_table(table_hbm, my_sect, other_core, 1)]
    chunks = []
    for k in range(vars_):
        lat = pl.ds(to_var[(k + 1) % vars_] * per, per)
        group = []
        for d in range(1, sects):
            at = pl.ds(pl.multiple_of(to_sect[d] * cols, cols), cols)
            copy = pltpu.make_async_remote_copy(
                src_ref=patches.at[lat, at, :],
                dst_ref=patch_in.at[d - 1, lat],
                send_sem=patch_send.at[k, d],
                recv_sem=patch_recv.at[k, d],
                device_id={"sect": to_sect[d]},
                device_id_type=MESH,
            )
            copy.start()
            group.append(copy)
        chunks.append(group)
    lines = gains.shape[0]
    params_in[my_var, :lines] = gains[...]
    params_in[my_var, lines:] = biases[...]
    for d in range(1, vars_):
        own = params_in.at[my_var]
        later.append(send(own, own, sems, 2, d, "var", to_var[d]))
    stack_rows = stack.shape[1]
    half = stack_rows - w_out.shape[1]
    carried = []
    for layer in range(layers):
        halves = [
            spread(
                stack.at[layer, at], others.at[layer, :, at],
                spread_send.at[layer, k], spread_recv.at[layer, k], k == 0,
            )
            for k, at in enumerate((slice(0, half), slice(half, stack_rows)))
        ]
        carried.append(halves)
    for load in loads[:3]:
        load.wait()
    advance(carried[0][0], 0)
    tables[0].wait()
    relayed = pass_table(table_in.at[sects // 2 - 1], other_chip, other_core, 2)
    for load in loads[3:]:
        load.wait()
    tables[1].wait()
    relayed.wait()
    weights = jnp.concatenate([table[...]] + [table_in[d] for d in range(sects - 1)], axis=0)

    def partial_of(owner):
        lat = pl.ds(owner * per, per)
        own = own_patch[lat]
        blocks = [own] + [patch_in[d, lat] for d in range(sects - 1)]
        x = jnp.concatenate([block.reshape(rows, depth) for block in blocks], axis=1)
        return dot(x, weights)

    outgoing = []
    for d in range(1, vars_):
        for copy in chunks[d - 1]:
            copy.wait()
        part[d - 1] = partial_of(to_var[d]).astype(jnp.bfloat16)
        outgoing.append(
            send(part.at[d - 1], part_in.at[d - 1], sems, 3, d, "var", to_var[d])
        )
    advance(carried[0][0], 1)
    advance(carried[0][1], 0)
    for copy in chunks[vars_ - 1]:
        copy.wait()
    total = partial_of(my_var)
    for d in range(1, vars_):
        outgoing[d - 1].wait()
        total = total + part_in[d - 1].astype(jnp.float32)
    full[0, my_var] = total.astype(jnp.bfloat16)
    for d in range(1, sects):
        later.append(send(decode, decode_in.at[d - 1], sems, last, d, "sect", to_sect[d]))
    advance(carried[0][0], 2)
    advance(carried[0][1], 1)
    for layer in range(layers):
        gather_project(
            full.at[layer], wqkv.at[layer], q_ref, kv_ref.at[layer], sems, 7 + 4 * layer,
            (halo_send.at[layer], halo_recv.at[layer]),
        )
        if layer == 0:
            for copy in later:
                copy.wait()
        early, late = carried[layer]
        ahead = carried[layer + 1] if layer + 1 < layers else []
        advance(early, 3)
        advance(late, 3 if layer else 2)
        for half_gather in ahead:
            advance(half_gather, 0)
        attention(
            layer, shifts, scales, q_ref, kv_ref.at[layer], wide, q_shifted, kv_shifted,
            framed, attended.at[layer],
        )
        feed(
            layer, attended.at[layer], attended_in.at[layer], stack.at[layer], others.at[layer],
            params_in, full.at[layer], full.at[layer + 1], sems, 4 + 4 * layer,
            ([(early, 4)], [(half_gather, 1) for half_gather in ahead] + ([] if layer else [(late, 3)]), [(late, 4)]),
        )
        for half_gather in ahead:
            advance(half_gather, 2)
    stream = full.at[layers]
    outgoing = [
        send(stream.at[my_var], stream.at[my_var], sems, last + 1, d, "var", to_var[d])
        for d in range(1, vars_)
    ]
    weights = jnp.concatenate([decode[...]] + [decode_in[d] for d in range(sects - 1)], axis=1)
    copies = []
    for k in range(vars_):
        if k:
            outgoing[k - 1].wait()
        lat = pl.ds(from_var[k] * per, per)
        decoded = dot(stream[from_var[k]], weights).astype(jnp.bfloat16)
        for d in range(sects):
            block = decoded[:, d * depth : (d + 1) * depth].reshape(per, cols, depth)
            made[d, lat] = block
            if d:
                copies.append(
                    send(
                        made.at[d, lat], landed.at[sects - d, lat], sems, last + 2 + k, d, "sect",
                        from_sect[d],
                    )
                )
    out_ref[:, pl.ds(pl.multiple_of(my_sect * cols, cols), cols), :] = made[0]
    for copy in copies:
        copy.wait()
    for d in range(1, sects):
        at = pl.ds(pl.multiple_of(to_sect[d] * cols, cols), cols)
        out_ref[:, at, :] = landed[sects - d]


def per_device(
    patches,
    embed_weight,
    qkv_weight,
    out_weight,
    mlp_in_weight,
    mlp_out_weight,
    logit_scale,
    norm_gain,
    norm_bias,
    decode_weight,
    shifts,
):
    _, lat_rows, lon_total, patch_dim = patches.shape
    width = embed_weight.shape[2]
    layers, _, _, head_cols = qkv_weight.shape
    sects, vars_ = lax.axis_size("sect"), lax.axis_size("var")
    cols = lon_total // sects
    tokens = lat_rows * cols
    rows = tokens // vars_
    bf = jnp.bfloat16
    vmem = pl.BlockSpec(memory_space=pltpu.VMEM)
    smem = pl.BlockSpec(memory_space=pltpu.SMEM)
    hbm = pl.BlockSpec(memory_space=pltpu.HBM)
    wqkv = qkv_weight.transpose(0, 2, 1, 3)
    gains, biases = norm_gain.reshape(2 * layers, -1), norm_bias.reshape(2 * layers, -1)
    stack_rows = out_weight.shape[1] + mlp_in_weight.shape[1] + mlp_out_weight.shape[1]
    shards = pltpu.VMEM((vars_ - 1, rows, width), bf)
    ext_rows, ext_cols = lat_rows + 2 * WL, cols + 2 * WW
    phases = 4 + 4 * layers + 2 + vars_
    scratch = [
        pltpu.VMEM((lat_rows, cols, patch_dim), bf),
        pltpu.VMEM((patch_dim, width), bf),
        pltpu.VMEM((layers, 3, width, head_cols), bf),
        pltpu.VMEM((width, patch_dim), bf),
        pltpu.SemaphoreType.DMA((8,)),
        pltpu.VMEM((layers, stack_rows, width), bf),
        pltpu.VMEM((sects - 1, lat_rows, cols, patch_dim), bf),
        pltpu.VMEM((sects - 1, patch_dim, width), bf),
        pltpu.VMEM((vars_, 4 * layers, gains.shape[1]), jnp.float32),
        shards,
        shards,
        pltpu.VMEM((layers + 1, vars_, rows, width), bf),
        pltpu.VMEM((layers, vars_ - 1, stack_rows, width), bf),
        pltpu.VMEM((layers, vars_ - 1, rows, head_cols), bf),
        pltpu.VMEM((ext_rows, ext_cols, head_cols), jnp.float32),
        pltpu.VMEM((layers, ext_rows, ext_cols, 2 * head_cols), bf),
        pltpu.VMEM((ext_rows, ext_cols, 2 * head_cols), jnp.float32),
        pltpu.VMEM((lat_rows + WL, cols + WW, head_cols), bf),
        pltpu.VMEM((lat_rows + WL, cols + WW, 2 * head_cols), bf),
        pltpu.VMEM((lat_rows + WL, cols + WW, head_cols), jnp.float32),
        pltpu.VMEM((layers, tokens, head_cols), bf),
        pltpu.VMEM((sects - 1, width, patch_dim), bf),
        pltpu.VMEM((sects, lat_rows, cols, patch_dim), bf),
        pltpu.VMEM((sects, lat_rows, cols, patch_dim), bf),
        pltpu.SemaphoreType.DMA((phases, 4)),
        pltpu.SemaphoreType.DMA((phases, 4)),
        pltpu.SemaphoreType.DMA((layers, vars_, 8)),
        pltpu.SemaphoreType.DMA((layers, vars_, 8)),
        pltpu.SemaphoreType.DMA((layers, 2, vars_ + 2)),
        pltpu.SemaphoreType.DMA((layers, 2, vars_ + 2)),
        pltpu.SemaphoreType.DMA((vars_, sects)),
        pltpu.SemaphoreType.DMA((vars_, sects)),
    ]
    out = pl.pallas_call(
        whole_kernel,
        out_shape=jax.ShapeDtypeStruct((lat_rows, lon_total, patch_dim), bf),
        in_specs=[hbm] * 6 + [smem, vmem, vmem, hbm, smem],
        out_specs=vmem,
        scratch_shapes=scratch,
        compiler_params=pltpu.CompilerParams(
            collective_id=0, has_side_effects=True, vmem_limit_bytes=64 * 1024 * 1024 - 65536
        ),
    )(
        patches[0], embed_weight[0], wqkv, out_weight, mlp_in_weight, mlp_out_weight,
        logit_scale, gains, biases, decode_weight[0], shifts,
    )
    return out[None]


def solution(mesh):
    return jax.shard_map(
        per_device,
        mesh=mesh,
        in_specs=(
            P(("sect", "var"), "lat", None, None),
            P(("sect", "var"), None, None),
            P(None, None, None, "var"),
            P(None, "var", None),
            P(None, None, "var"),
            P(None, "var", None),
            P(None, "var"),
            P(None, None, "var"),
            P(None, None, "var"),
            P(("sect", "var"), None, None),
            P(),
        ),
        out_specs=P(("sect", "var"), "lat", None, None),
        check_vma=False,
    )
```
